512 devices in a mesh: expert: 128 (over z, y, core), section: 4 (over x).
Axes of the slice: x: 4, y: 8, z: 8, core: 2. Of those that a mesh axis runs over, the one named last changes fastest.
Arguments:
- prev_out: bfloat16 [4, 1024, 3584], P('section', 'expert'), may hold values from -6 to 6
- next_grad: bfloat16 [4, 1024, 3584], P('section', 'expert'), may hold values from -3 to 3
- expert_ids: int32 [4, 1024, 8], P('section', 'expert'), may hold values from 0 to 15, all different within a row; in each aligned block of 8 rows (0 to 7, 8 to 15, ..., all dimensions but the last counted through in order) at most 5 rows name the same one
- affinity: float32 [4, 1024, 8], P('section', 'expert'), may hold values from 0.2 to 1
- w_gate_up: bfloat16 [4, 128, 3584, 256], P('section', 'expert'), may hold values from -0.09375 to 0.09375
- w_down: bfloat16 [4, 128, 128, 3584], P('section', 'expert'), may hold values from -0.1875 to 0.1875
Outputs:
- input_grad: bfloat16 [4, 1024, 3584], P('section', 'expert')
- grad_down: bfloat16 [4, 128, 128, 3584], P('section', 'expert')
- score_grad: float32 [4, 1024, 8], P('section', 'expert')
The draws below stay inside these ranges and needn't reach their ends.
Inputs may be any that keep to these rules, and one draw needn't show every extreme that they name: `expert_ids`: in each section the 8 tokens of one device, each naming 8 different experts, name any one expert at most 5 times.
All inputs are finite; a program needn't handle non-finite values.
Results may differ from the reference program's by a relative error of at most 0.013.
Values may be sent and summed in bfloat16 or wider, within the bound.
A program may use at most 128 MiB of HBM per device.

```python
import math
import jax
import jax.numpy as jnp
import numpy as np
from jax import lax

D = 3584
HID = 1024
TOP = 8
TOK_DEV = 8
EXPERTS = 16
SPLIT = 8
HS = 128
SECTIONS = 4
TOKENS = 1024
CAP = 5
N_EXPERT = 128


def block_levels(stream_key, dims, split, low, high):
    def one(dim, shards_of):
        steps = jax.random.uniform(jax.random.fold_in(jax.random.fold_in(stream_key, 6), dim), (shards_of,), jnp.float32, low / len(split), high / len(split))
        return jnp.repeat(jnp.exp(steps), dims[dim] // shards_of).reshape((-1,) + (1,) * (len(dims) - dim - 1))

    gain = one(*split[0])
    for cut in split[1:]:
        gain = gain * one(*cut)
    return gain


def assign_block(own_key, own, number, rows, amount, top, limit, skew):
    ranking = jax.random.permutation(own_key, amount)
    crowded, usual = shares(amount, rows * top, limit, skew, True), shares(amount, rows * top, limit, skew, False)
    places = jnp.arange(amount)

    def named(sizes, rotation):
        used = int((sizes > 0).sum())
        fixed = max(1, used // 4)
        moved = fixed + (places - fixed + rotation * (used - fixed)) % max(1, amount - fixed)
        return jnp.zeros((amount,), jnp.int32).at[ranking[jnp.where(places < fixed, places, moved)]].set(jnp.asarray(sizes, jnp.int32))

    sizes = jnp.where(number % 4 == 0, named(crowded, number // 4), named(usual, number - number // 4 - 1))
    mixed = jax.random.permutation(jax.random.fold_in(own, 3), amount)
    giver, taker = mixed[0:amount // 2 * 2:2], mixed[1:amount // 2 * 2:2]
    margin = jnp.minimum(sizes[giver] - 1, limit - sizes[taker]) // 2
    margin = jnp.where((giver == ranking[0]) | (taker == ranking[0]) | (sizes[taker] == 0), 0, jnp.maximum(margin, 0))
    moved = jax.random.randint(jax.random.fold_in(own, 4), (amount // 2,), 0, 1 << 20) % (margin + 1)
    sizes = sizes.at[giver].add(-moved).at[taker].add(moved)
    members = jnp.searchsorted(jnp.cumsum(sizes), jnp.arange(rows * top), side="right").astype(jnp.int32)
    listing = members.reshape(top, rows).T
    listing = listing[jax.random.permutation(jax.random.fold_in(own, 1), rows)]
    rotation = jax.random.randint(jax.random.fold_in(own, 2), (rows, 1), 0, top)
    return jnp.take_along_axis(listing, (jnp.arange(top)[None, :] + rotation) % top, axis=1)


def shares(count, total, reach, skew, full):
    portions = [(1 << 20) // math.isqrt(rank ** skew) + 1 for rank in range(1, count + 1)]
    largest = reach if full else min(reach, max(-(-total // count), total * portions[0] // sum(portions)))
    least = 1 if total - largest >= count - 1 else 0
    given, spare = [largest] + [least] * (count - 1), total - largest - least * (count - 1)
    while spare > 0:
        candidates = [i for i in range(1, count) if given[i] < largest] or [i for i in range(1, count) if given[i] < reach]
        mass, left = sum([portions[i] for i in candidates]), spare
        for i in candidates:
            more = min(reach - given[i], max(1, left * portions[i] // mass), spare)
            given[i] = given[i] + more
            spare = spare - more
    return np.array(given)


def centred(stream_key, shape, width, reach, cuts=(), kind=jnp.bfloat16):
    values = width * jax.random.normal(stream_key, shape, jnp.float32)
    if cuts:
        values = values * block_levels(stream_key, shape, cuts, -0.22, 0.18)
    return jnp.clip(values, -reach, reach).astype(kind)


def setup_inputs(seed: int = 0) -> dict:
    arg_keys = jax.random.split(jax.random.key(seed), 7)
    prev_out = centred(arg_keys[0], (SECTIONS, TOKENS, D), 1.0, 6.0, ((0, 4), (1, 128)))
    next_grad = centred(arg_keys[1], (SECTIONS, TOKENS, D), 0.5, 3.0, ((0, 4), (1, 128)))
    expert_ids_keys = jax.random.split(jax.random.fold_in(arg_keys[2], 1), SECTIONS * TOKENS // TOK_DEV)
    expert_ids_turns = jax.random.permutation(jax.random.fold_in(arg_keys[2], 3), SECTIONS * TOKENS // TOK_DEV)
    expert_ids = jax.vmap(lambda own, number: assign_block(jax.random.fold_in(arg_keys[2], 2), own, number, TOK_DEV, EXPERTS, TOP, CAP, 2))(expert_ids_keys, expert_ids_turns).reshape((SECTIONS, TOKENS, TOP))
    affinity = jnp.clip(jnp.exp(math.log(1.0) - 1.609438 * jax.random.uniform(arg_keys[3], (SECTIONS, TOKENS, TOP), jnp.float32) ** block_levels(arg_keys[3], (SECTIONS, TOKENS, TOP), ((0, 4), (1, 128)), -0.2, 0.2)), 0.2, 1.0)
    w_gate_up = centred(arg_keys[4], (SECTIONS, N_EXPERT, D, 2 * HS), D ** -0.5, 0.09375, ((0, 4), (1, 128)))
    w_down = centred(arg_keys[5], (SECTIONS, N_EXPERT, HS, D), HID ** -0.5, 0.1875, ((0, 4), (1, 128)))
    return dict(prev_out=prev_out, next_grad=next_grad, expert_ids=expert_ids, affinity=affinity, w_gate_up=w_gate_up, w_down=w_down)


def slice_pass(rows_x, rows_g, w_in, w_out):
    units = w_out.shape[0]
    gate_up = jnp.dot(rows_x, w_in, preferred_element_type=jnp.float32)
    a_part = gate_up[:, :units]
    b_part = gate_up[:, units:]
    sigmoid_a = jax.nn.sigmoid(a_part)
    active = a_part * sigmoid_a
    hidden = (active * b_part).astype(jnp.bfloat16)
    q_rows = lax.dot_general(rows_g, w_out, (((1,), (1,)), ((), ())), preferred_element_type=jnp.float32)
    r_rows = jnp.sum(hidden.astype(jnp.float32) * q_rows, axis=1).astype(jnp.bfloat16)
    grad_ab = jnp.concatenate([q_rows * b_part * sigmoid_a * (1.0 + a_part * (1.0 - sigmoid_a)), q_rows * active], axis=1).astype(jnp.bfloat16)
    dx_rows = lax.dot_general(grad_ab, w_in, (((1,), (1,)), ((), ())), preferred_element_type=jnp.float32).astype(jnp.bfloat16)
    grad_dn = lax.dot_general(hidden, rows_g, (((0,), (0,)), ((), ())), preferred_element_type=jnp.float32).astype(jnp.bfloat16)
    return dx_rows, r_rows, grad_dn


def reference(prev_out, next_grad, expert_ids, affinity, w_gate_up, w_down):
    sections = prev_out.shape[0]
    grads_in, grads_dn, grads_score = [], [], []
    for section in range(sections):
        x_in = prev_out[(section - 1) % sections]
        dy_in = next_grad[(section + 1) % sections]
        chosen_ids = expert_ids[section]
        chosen = affinity[section]
        tokens, top = chosen_ids.shape
        blocks = chosen_ids.reshape(N_EXPERT, TOK_DEV * top)
        onehot = (blocks[:, :, None] == jnp.arange(EXPERTS, dtype=jnp.int32)[None, None, :]).astype(jnp.int32)
        rank = jnp.cumsum(onehot, axis=1, dtype=jnp.int32) - 1
        slot = jnp.sum(rank * onehot, axis=2, dtype=jnp.int32)
        owner = jnp.broadcast_to(jnp.arange(N_EXPERT, dtype=jnp.int32)[:, None], blocks.shape)
        flat = jnp.arange(tokens * top, dtype=jnp.int32).reshape(blocks.shape)
        table = jnp.full((EXPERTS, N_EXPERT, CAP), tokens * top, jnp.int32).at[blocks, owner, slot].set(flat)
        total = jnp.sum(chosen, axis=1)
        weight = chosen / total[:, None]
        x_pad = jnp.concatenate([x_in, jnp.zeros((1, D), jnp.bfloat16)], axis=0)
        dy_pad = jnp.concatenate([dy_in, jnp.zeros((1, D), jnp.bfloat16)], axis=0)
        weight_pad = jnp.concatenate([weight.reshape(-1), jnp.zeros((1,), jnp.float32)])

        def per_slice(carry, item):
            dx_acc, r_acc = carry
            index, w_in, w_out = item
            table_e = lax.dynamic_index_in_dim(table, (index // SPLIT).astype(jnp.int32), 0, keepdims=False)
            route = table_e.reshape(-1)
            token = (route // top).astype(jnp.int32)
            rows_x = x_pad[token]
            rows_g = (weight_pad[route][:, None] * dy_pad[token].astype(jnp.float32)).astype(jnp.bfloat16)
            dx_rows, r_rows, grad_dn = slice_pass(rows_x, rows_g, w_in, w_out)
            r_rows = lax.optimization_barrier(r_rows)
            dx_acc = dx_acc.at[token].add(dx_rows.astype(jnp.float32))
            r_acc = r_acc.at[route].add(r_rows.astype(jnp.float32))
            return (dx_acc, r_acc), grad_dn

        init = (jnp.zeros((tokens + 1, D), jnp.float32), jnp.zeros((tokens * top + 1,), jnp.float32))
        items = (jnp.arange(N_EXPERT, dtype=jnp.int32), w_gate_up[section], w_down[section])
        (dx_acc, r_acc), grad_dn = lax.scan(per_slice, init, items)
        r_val = r_acc[:tokens * top].reshape(tokens, top)
        grads_in.append(dx_acc[:tokens].astype(jnp.bfloat16))
        grads_dn.append(grad_dn)
        grads_score.append(r_val / chosen - jnp.sum(r_val, axis=1, keepdims=True) / total[:, None])
    return jnp.stack(grads_in), jnp.stack(grads_dn), jnp.stack(grads_score)
```

```python
import functools

import jax
import jax.numpy as jnp
from jax import lax
from jax.experimental import pallas as pl
from jax.experimental.pallas import tpu as pltpu
from jax.sharding import PartitionSpec as P

MESH = pl.DeviceIdType.MESH
F32 = jnp.float32
BF16 = jnp.bfloat16
LANES = 128
VMEM_BYTES = 60 * 1024 * 1024


def wrap(value, length):
    return lax.rem(value + length, length)


def order_of(index, length):
    if isinstance(index, int):
        return (length - index) // 2, 1 - 2 * (index % 2)
    return lax.div(length - index, 2), 1 - 2 * lax.rem(index, 2)


def place(index, centre, length):
    hops, sign = order_of(index, length)
    return wrap(centre + sign * hops, length)


def kernel(
    R,
    sections,
    split,
    x_ref,
    g_ref,
    ids_ref,
    aff_ref,
    win_hbm,
    wout_hbm,
    dx_out,
    gd_out,
    sg_out,
    buf,
    win,
    wout,
    shift_src,
    shift_dst,
    wt_src,
    wt_dst,
    ab,
    qb,
    gab,
    hw,
    rb,
    acc,
    pair_src,
    pair_dst,
    ring_src,
    ring_dst,
    line_src,
    line_dst,
    fin_src,
    fin_dst,
    load_sem,
    shift_send,
    shift_recv,
    wt_sem,
    a_send,
    a_recv,
    b_send,
    b_recv,
    sib_send,
    sib_recv,
    pair_send,
    pair_recv,
    ring_send,
    ring_recv,
    line_send,
    line_recv,
    fin_sem,
):
    half = R // 2
    rows, D = x_ref.shape
    H = D // 2
    block = 2 * rows
    units = wout.shape[0]
    top = ids_ref.shape[1]
    per = ring_src.shape[3]
    groups = R // per
    me = lax.axis_index("expert")
    sec = lax.axis_index("section")
    c = lax.rem(me, 2)
    chip = lax.div(me, 2)
    z, y = lax.div(chip, R), lax.rem(chip, R)
    a = y + c * (z - y)
    b = z + c * (y - z)
    expert = lax.div(me, split)
    sec_next, sec_prev = wrap(sec + 1, sections), wrap(sec - 1, sections)

    def at(a_pos, b_pos):
        z_pos = b_pos + c * (a_pos - b_pos)
        y_pos = a_pos + c * (b_pos - a_pos)
        return {"expert": (z_pos * R + y_pos) * 2 + c, "section": sec}

    a_next, a_prev = at(wrap(a + 1, R), b), at(wrap(a - 1, R), b)
    b_next, b_prev = at(a, wrap(b + 1, R)), at(a, wrap(b - 1, R))
    sibling = {"expert": chip * 2 + 1 - c, "section": sec}

    def remote(src, dst, send, recv, device):
        return pltpu.make_async_remote_copy(
            src_ref=src, dst_ref=dst, send_sem=send, recv_sem=recv, device_id=device, device_id_type=MESH
        )

    load_in = pltpu.make_async_copy(win_hbm, win, load_sem.at[0])
    load_out = pltpu.make_async_copy(wout_hbm, wout, load_sem.at[1])
    load_in.start()
    load_out.start()

    barrier = pltpu.get_barrier_semaphore()
    source = wrap(sec - 1 + 2 * c, sections)
    for device in (
        a_next,
        a_prev,
        b_next,
        b_prev,
        sibling,
        {"expert": chip * 2, "section": source},
        {"expert": chip * 2 + 1, "section": source},
    ):
        pl.semaphore_signal(barrier, inc=1, device_id=device, device_id_type=MESH)

    def packed(value):
        wide = value.astype(F32)
        return jnp.concatenate([wide[:, :H], wide[:, H:]], axis=0).astype(BF16)

    shift_src[0] = packed(x_ref[...])
    shift_src[1] = packed(g_ref[...])
    chosen = aff_ref[...]
    ids = ids_ref[...]
    total = jnp.sum(chosen, axis=1, keepdims=True)
    weight = chosen / total
    lane8 = lax.broadcasted_iota(jnp.int32, (rows, LANES), 1)
    dense = jnp.zeros((rows, LANES), F32)
    for k in range(top):
        dense = dense + jnp.where(lane8 == ids[:, k : k + 1], weight[:, k : k + 1], 0.0)
    wt_src[...] = dense
    pl.semaphore_wait(barrier, 7)

    send_x = remote(
        shift_src.at[0], shift_dst.at[c], shift_send.at[0], shift_recv.at[c], {"expert": chip * 2, "section": sec_next}
    )
    send_g = remote(
        shift_src.at[1], shift_dst.at[c], shift_send.at[1], shift_recv.at[c], {"expert": chip * 2 + 1, "section": sec_prev}
    )
    send_w = remote(wt_src, wt_dst, wt_sem.at[0], wt_sem.at[1], sibling)
    send_x.start()
    send_g.start()
    send_w.start()
    for i in range(2):
        remote(shift_src.at[0], shift_dst.at[i], shift_send.at[0], shift_recv.at[i], sibling).wait_recv()
    send_w.wait_recv()
    low, high = shift_dst[0].astype(F32), shift_dst[1].astype(F32)
    mine, other = wt_src[...], wt_dst[...]
    pair_wt = jnp.concatenate([jnp.where(c == 0, mine, other), jnp.where(c == 0, other, mine)], axis=0)
    lead = pair_wt.astype(BF16).astype(F32)
    buf[c, b, a, :, 0:H] = jnp.concatenate([low[:rows], high[:rows]], axis=0).astype(BF16)
    buf[c, b, a, :, H:D] = jnp.concatenate([low[rows:], high[rows:]], axis=0).astype(BF16)
    buf[c, b, a, :, D:] = jnp.where(c == 0, lead, pair_wt - lead).astype(BF16)

    def along_a(j, way, hop):
        return remote(
            buf.at[c, b, j], buf.at[c, b, j], a_send.at[way, hop], a_recv.at[way, hop], a_next if way == 0 else a_prev
        )

    def along_b(origin, j, way, hop, piece):
        return remote(
            buf.at[c, origin, j],
            buf.at[c, origin, j],
            b_send.at[way, hop],
            b_recv.at[way, hop, piece],
            b_next if way == 0 else b_prev,
        )

    def to_sibling(origin, j):
        return remote(buf.at[c, origin, j], buf.at[c, origin, j], sib_send.at[origin], sib_recv.at[origin], sibling)

    for o in range(R):
        hops, sign = order_of(R - 1 - o, R)
        j = wrap(a + sign * hops, R)
        if o == 0:
            if half > 1:
                along_a(j, 0, 1).start()
            along_a(j, 1, 1).start()
        elif sign > 0:
            along_a(j, 1, hops).wait_recv()
            if hops < half:
                along_a(j, 1, hops + 1).start()
        else:
            along_a(j, 0, hops).wait_recv()
            if hops < half - 1:
                along_a(j, 0, hops + 1).start()
        if half > 1 or o < half:
            along_b(b, j, 0, 1, o).start()
        if half > 1 or o >= half:
            along_b(b, j, 1, 1, o).start()
        to_sibling(b, j).start()

    def forward(hop, o, carry):
        j = place(R - 1 - o, a, R)
        left, right = wrap(b - (hop - 1), R), wrap(b + (hop - 1), R)
        along_b(left, j, 0, hop - 1, o).wait_recv()
        if hop < half:
            along_b(left, j, 0, hop, o).start()
        else:

            @pl.when(o < half)
            def _():
                along_b(left, j, 0, hop, o).start()

        to_sibling(left, j).start()
        along_b(right, j, 1, hop - 1, o).wait_recv()
        if hop < half:
            along_b(right, j, 1, hop, o).start()
        else:

            @pl.when(o >= half)
            def _():
                along_b(right, j, 1, hop, o).start()

        to_sibling(right, j).start()
        return carry

    def wait_sibling(origin):
        remote(buf.at[1 - c, origin], buf.at[1 - c, origin], sib_send.at[origin], sib_recv.at[origin], sibling).wait_recv()

    def project(z_slab, y_slab):
        rows_lo = buf[0, z_slab, :, :, 0:H].reshape(R * block, H)
        rows_hi = buf[0, z_slab, :, :, H:D].reshape(R * block, H)
        ab[z_slab] = jnp.dot(rows_lo, win[0], preferred_element_type=F32) + jnp.dot(
            rows_hi, win[1], preferred_element_type=F32
        )
        rows_g = buf[1, y_slab, :, :, 0:D].reshape(R * block, D)
        q = lax.dot_general(rows_g, wout[...], (((1,), (1,)), ((), ())), preferred_element_type=F32)
        qb[:, y_slab] = q.reshape(R, block, units)

    def project_at(distance):
        if distance == 0 or distance == half:
            wait_sibling(wrap(a + distance, R))
            project(wrap(z + distance, R), wrap(y + distance, R))
        else:

            def side(i, carry):
                step = distance * (1 - 2 * i)
                wait_sibling(wrap(a + step, R))
                project(wrap(z + step, R), wrap(y + step, R))
                return carry

            lax.fori_loop(0, 2, side, 0)

    for hop in range(2, half + 1):
        lax.fori_loop(0, R, functools.partial(forward, hop), 0)
        if hop == 2:
            load_in.wait()
            load_out.wait()
        project_at(hop - 2)
    if half == 1:
        load_in.wait()
        load_out.wait()
    project_at(half - 1)
    far = wrap(b + half, R)

    def last(o, carry):
        j = place(R - 1 - o, a, R)
        along_b(far, j, 0, half, o).wait_recv()
        to_sibling(far, j).start()
        j = place(R - 1 - (o + half), a, R)
        along_b(far, j, 1, half, o + half).wait_recv()
        to_sibling(far, j).start()
        return carry

    lax.fori_loop(0, half, last, 0)
    project_at(half)

    def activate(z_slab, carry):
        lane = lax.broadcasted_iota(jnp.int32, (R * block, LANES), 1)
        wt = buf[0, z_slab, :, :, D:].astype(F32) + buf[1, :, z_slab, :, D:].astype(F32)
        w = jnp.sum(jnp.where(lane == expert, wt.reshape(R * block, LANES), 0.0), axis=1, keepdims=True)
        a_part = ab[z_slab, :, 0:units]
        b_part = ab[z_slab, :, units:]
        q = qb[z_slab].reshape(R * block, units) * w
        sig = jax.nn.sigmoid(a_part)
        active = a_part * sig
        hidden = active * b_part
        r = jnp.sum(hidden.astype(BF16).astype(F32) * q, axis=1, keepdims=True)
        gab[z_slab, :, :, 0:units] = (
            (q * b_part * sig * (1.0 + a_part * (1.0 - sig))).astype(BF16).reshape(R, block, units)
        )
        gab[z_slab, :, :, units:] = (q * active).astype(BF16).reshape(R, block, units)
        hw[:, z_slab] = (hidden * w).astype(BF16).reshape(R, block, units)
        rb[z_slab] = jnp.where(lane == expert, r, 0.0).astype(BF16).reshape(R, block, LANES)
        return carry

    lax.fori_loop(0, R, activate, 0)

    def spot(target, j, swap):
        return target + swap * (j - target), j + swap * (target - j)

    def products(target, centre, swap, h):
        parts = []
        for u in range(R):
            zi, yi = spot(target, place(u, centre, R), swap)
            parts.append(gab[zi, yi])
        rows_ab = jnp.concatenate(parts, axis=0)
        return lax.dot_general(rows_ab, win[h], (((1,), (1,)), ((), ())), preferred_element_type=F32)

    def pair_copy(n):
        return remote(pair_src.at[n], pair_dst.at[n], pair_send.at[n], pair_recv.at[n], sibling)

    def give(n):
        value = products(place(n, a, R), b, 1 - c, 1 - c)
        pair_src[n] = value.astype(BF16).reshape(R, block, H)
        pair_copy(n).start()

    def ring_copy(way, hop, g):
        return remote(
            ring_src.at[way, hop, g],
            ring_dst.at[way, hop, g],
            ring_send.at[way, hop],
            ring_recv.at[way, hop, g],
            b_next if way == 0 else b_prev,
        )

    def wait_ring(way, hop, g):
        ring_copy(way, hop, g).wait_recv()

    def dense_r(target, g):
        parts = []
        for i in range(per):
            zi, yi = spot(target, place(g * per + i, a, R), c)
            parts.append(rb[zi, yi].astype(F32)[None])
        return jnp.concatenate(parts, axis=0)

    def keep(n):
        acc[...] = products(place(n, b, R), a, c, c).reshape(groups, per, block, H)
        pair_copy(n).wait_recv()

    def local_sum(n, g):
        value = acc[g] + pair_dst[n, pl.ds(g * per, per)].astype(F32)
        return value, dense_r(place(n, b, R), g)

    def send_on(way, hop, g, value, r_value):
        ring_src[way, hop, g, :, :, 0:H] = value.astype(BF16)
        ring_src[way, hop, g, :, :, H:] = r_value.astype(BF16)

    def start_ring(hop, g, sign):
        @pl.when(sign > 0)
        def _():
            ring_copy(0, hop, g).start()

        @pl.when(sign < 0)
        def _():
            ring_copy(1, hop, g).start()

    give(0)
    if R > 1:
        give(1)

    keep(0)
    give(min(2, R - 1)) if R > 2 else None
    for g in range(groups):
        way = 0 if g < groups // 2 else 1
        value, r_value = local_sum(0, g)
        send_on(way, half, g, value, r_value)
        ring_copy(way, half, g).start()

    def relay(partial, n, carry):
        hops, sign = order_of(n, R)
        way = lax.rem(n, 2)
        keep(n)

        @pl.when(n + 2 < R)
        def _():
            give(n + 2)

        def group(g, carry):
            value, r_value = local_sum(n, g)

            def with_arrived():
                back = ring_dst.at[way, hops + 1, g]
                remote(
                    back, back, ring_send.at[way, hops + 1], ring_recv.at[way, hops + 1, g], sibling
                ).wait_recv()
                arrived = back[...].astype(F32)
                send_on(way, hops, g, value + arrived[:, :, 0:H], r_value + arrived[:, :, H:])

            if partial:
                here = lax.div(g, groups // 2) == way

                @pl.when(here)
                def _():
                    with_arrived()

                @pl.when(jnp.logical_not(here))
                def _():
                    send_on(way, hops, g, value, r_value)

            else:
                with_arrived()
            start_ring(hops, g, sign)
            return carry

        lax.fori_loop(0, groups, group, 0)
        return carry

    if R > 2:
        lax.fori_loop(1, 3, functools.partial(relay, True), 0)
    if R > 4:
        lax.fori_loop(3, R - 1, functools.partial(relay, False), 0)

    def line_copy(way, hop):
        return remote(
            line_src.at[way, hop],
            line_dst.at[way, hop],
            line_send.at[way, hop],
            line_recv.at[way, hop],
            a_next if way == 0 else a_prev,
        )

    chunk = D // 7 if D % (7 * LANES) == 0 else LANES
    chunks = D // chunk

    def grad_down(i):
        cols = pl.ds(pl.multiple_of(i * chunk, chunk), chunk)
        g_rows = buf[1, :, :, :, cols].reshape(R * R * block, chunk)
        h_rows = hw[...].reshape(R * R * block, units)
        gd_out[:, cols] = lax.dot_general(
            h_rows, g_rows, (((0,), (0,)), ((), ())), preferred_element_type=F32
        ).astype(BF16)

    n = R - 1
    keep(n)
    done = 0
    for g in range(groups):
        value, r_value = local_sum(n, g)
        for way in range(2):
            if half > 1 or (g < groups // 2) == (way == 0):
                wait_ring(way, 1, g)
                arrived = ring_dst[way, 1, g].astype(F32)
                value = value + arrived[:, :, 0:H]
                r_value = r_value + arrived[:, :, H:]
        for i in range(per):
            u = g * per + i
            hops, sign = order_of(u, R)
            v, rv = value[i], r_value[i]
            while done < chunks and done < (u + 1) * chunks // R:
                grad_down(done)
                done += 1
            ways = (0, 1) if hops == 0 else ((0,) if sign > 0 else (1,))
            for way in ways:
                if hops + 1 <= (half if way == 0 else half - 1):
                    line_copy(way, hops + 1).wait_recv()
                    arrived = line_dst[way, hops + 1].astype(F32)
                    v = v + arrived[:, 0:H]
                    rv = rv + arrived[:, H:]
            if hops > 0:
                way = ways[0]
                line_src[way, hops, :, 0:H] = v.astype(BF16)
                line_src[way, hops, :, H:] = rv.astype(BF16)
                line_copy(way, hops).start()
            else:
                fin_src[:, 0:H] = jnp.where(c == 0, v[rows:], v[:rows])
                fin_src[:, H:] = jnp.where(c == 0, rv[rows:], rv[:rows])
                swap_rows = remote(fin_src, fin_dst, fin_sem.at[0], fin_sem.at[1], sibling)
                swap_rows.start()
                own_rows = jnp.where(c == 0, v[:rows], v[rows:])
                own_r = jnp.where(c == 0, rv[:rows], rv[rows:])
                swap_rows.wait_recv()
                their_rows = fin_dst[:, 0:H]
                r_all = own_r + fin_dst[:, H:]
                dx_out[:, 0:H] = jnp.where(c == 0, own_rows, their_rows).astype(BF16)
                dx_out[:, H:] = jnp.where(c == 0, their_rows, own_rows).astype(BF16)
                swap_rows.wait_send()

    column = lax.broadcasted_iota(jnp.int32, (rows, top), 1)
    r_val = jnp.zeros((rows, top), F32)
    for k in range(top):
        r_k = jnp.sum(jnp.where(lane8 == ids[:, k : k + 1], r_all, 0.0), axis=1, keepdims=True)
        r_val = r_val + jnp.where(column == k, r_k, 0.0)
    sg_out[...] = r_val / chosen - jnp.sum(r_val, axis=1, keepdims=True) / total

    send_x.wait_send()
    send_g.wait_send()
    send_w.wait_send()
    for hop in range(1, half + 1):
        if hop < half:
            along_a(a, 0, hop).wait_send()
        along_a(a, 1, hop).wait_send()
        for way in range(2):
            count = R if hop < half else half
            slab = buf.at[c, b, pl.ds(0, count)]
            remote(slab, slab, b_send.at[way, hop], b_recv.at[way, hop, 0], sibling).wait_send()
            parts = groups if hop < half else groups // 2
            sent = ring_src.at[way, hop, pl.ds(0, parts)]
            remote(sent, sent, ring_send.at[way, hop], ring_recv.at[way, hop, 0], sibling).wait_send()
        line_copy(0, hop).wait_send()
        if hop < half:
            line_copy(1, hop).wait_send()

    def settle(i, carry):
        remote(buf.at[c, i], buf.at[c, i], sib_send.at[i], sib_recv.at[i], sibling).wait_send()
        pair_copy(i).wait_send()
        return carry

    lax.fori_loop(0, R, settle, 0)


def side_of(devices):
    R = 1
    while 2 * R * R < devices:
        R += 1
    return R


def on_device(prev_out, next_grad, expert_ids, affinity, w_gate_up, w_down):
    slices = lax.axis_size("expert")
    sections = lax.axis_size("section")
    R = side_of(slices)
    rows, D = prev_out.shape[1:]
    top = expert_ids.shape[2]
    units = w_down.shape[2]
    H = D // 2
    block = 2 * rows
    split = slices // max(top, slices // 8)
    half = R // 2
    per = max(1, R // 4)
    groups = R // per
    vmem = pl.BlockSpec(memory_space=pltpu.VMEM)
    anywhere = pl.BlockSpec(memory_space=pl.ANY)
    dma = pltpu.SemaphoreType.DMA
    flops = 2 * slices * rows * D * units * 6
    dx, gd, sg = pl.pallas_call(
        functools.partial(kernel, R, sections, split),
        out_shape=(
            jax.ShapeDtypeStruct((rows, D), BF16),
            jax.ShapeDtypeStruct((units, D), BF16),
            jax.ShapeDtypeStruct((rows, top), F32),
        ),
        in_specs=[vmem, vmem, vmem, vmem, anywhere, anywhere],
        out_specs=(vmem, vmem, vmem),
        scratch_shapes=[
            pltpu.VMEM((2, R, R, block, D + LANES), BF16),
            pltpu.VMEM((2, H, 2 * units), BF16),
            pltpu.VMEM((units, D), BF16),
            pltpu.VMEM((2, block, H), BF16),
            pltpu.VMEM((2, block, H), BF16),
            pltpu.VMEM((rows, LANES), F32),
            pltpu.VMEM((rows, LANES), F32),
            pltpu.VMEM((R, R * block, 2 * units), F32),
            pltpu.VMEM((R, R, block, units), F32),
            pltpu.VMEM((R, R, block, 2 * units), BF16),
            pltpu.VMEM((R, R, block, units), BF16),
            pltpu.VMEM((R, R, block, LANES), BF16),
            pltpu.VMEM((groups, per, block, H), F32),
            pltpu.VMEM((R, R, block, H), BF16),
            pltpu.VMEM((R, R, block, H), BF16),
            pltpu.VMEM((2, half + 1, groups, per, block, H + LANES), BF16),
            pltpu.VMEM((2, half + 1, groups, per, block, H + LANES), BF16),
            pltpu.VMEM((2, half + 1, block, H + LANES), BF16),
            pltpu.VMEM((2, half + 1, block, H + LANES), BF16),
            pltpu.VMEM((rows, H + LANES), F32),
            pltpu.VMEM((rows, H + LANES), F32),
            dma((2,)),
            dma((2,)),
            dma((2,)),
            dma((2,)),
            dma((2, half + 1)),
            dma((2, half + 1)),
            dma((2, half + 1)),
            dma((2, half + 1, R)),
            dma((R,)),
            dma((R,)),
            dma((R,)),
            dma((R,)),
            dma((2, half + 1)),
            dma((2, half + 1, groups)),
            dma((2, half + 1)),
            dma((2, half + 1)),
            dma((2,)),
        ],
        compiler_params=pltpu.CompilerParams(
            collective_id=0, has_side_effects=True, vmem_limit_bytes=VMEM_BYTES
        ),
        cost_estimate=pl.CostEstimate(flops=flops, bytes_accessed=4 * D * units * 2, transcendentals=0),
    )(
        prev_out[0],
        next_grad[0],
        expert_ids[0],
        affinity[0],
        w_gate_up[0, 0].reshape(2, H, 2 * units),
        w_down[0, 0],
    )
    return dx[None], gd[None, None], sg[None]


def solution(mesh):
    in_specs = (
        P("section", "expert", None),
        P("section", "expert", None),
        P("section", "expert", None),
        P("section", "expert", None),
        P("section", "expert", None, None),
        P("section", "expert", None, None),
    )
    out_specs = (
        P("section", "expert", None),
        P("section", "expert", None, None),
        P("section", "expert", None),
    )
    return jax.shard_map(
        on_device, mesh=mesh, in_specs=in_specs, out_specs=out_specs, check_vma=False
    )
```

```python
import functools

import jax
import jax.numpy as jnp
from jax import lax
from jax.experimental import pallas as pl
from jax.experimental.pallas import tpu as pltpu
from jax.sharding import PartitionSpec as P

MESH = pl.DeviceIdType.MESH
F32 = jnp.float32
BF16 = jnp.bfloat16
LANES = 128
LAG = 1
VMEM_BYTES = 60 * 1024 * 1024


def wrap(value, length):
    return lax.rem(value + length, length)


def order_of(index, length):
    if isinstance(index, int):
        return (length - index) // 2, 1 - 2 * (index % 2)
    return lax.div(length - index, 2), 1 - 2 * lax.rem(index, 2)


def place(index, centre, length):
    hops, sign = order_of(index, length)
    return wrap(centre + sign * hops, length)


def kernel(
    R,
    sections,
    split,
    x_hbm,
    g_hbm,
    ids_hbm,
    aff_hbm,
    win_hbm,
    wout_hbm,
    dx_out,
    gd_out,
    sg_out,
    x_ref,
    g_ref,
    ids_ref,
    aff_ref,
    buf,
    win,
    wout,
    shift_src,
    shift_dst,
    wt_src,
    wt_dst,
    ab,
    qb,
    gab,
    hw,
    rb,
    acc,
    pair_src,
    pair_dst,
    ring_src,
    ring_dst,
    line_src,
    line_dst,
    fin_src,
    fin_dst,
    load_sem,
    shift_send,
    shift_recv,
    wt_sem,
    a_send,
    a_recv,
    b_send,
    b_recv,
    sib_send,
    sib_recv,
    pair_send,
    pair_recv,
    ring_send,
    ring_recv,
    line_send,
    line_recv,
    fin_sem,
):
    half = R // 2
    rows, D = x_ref.shape
    H = D // 2
    block = 2 * rows
    units = wout.shape[0]
    top = ids_ref.shape[1]
    per = ring_src.shape[3]
    groups = R // per
    me = lax.axis_index("expert")
    sec = lax.axis_index("section")
    c = lax.rem(me, 2)
    chip = lax.div(me, 2)
    z, y = lax.div(chip, R), lax.rem(chip, R)
    a = y + c * (z - y)
    b = z + c * (y - z)
    expert = lax.div(me, split)
    sec_next, sec_prev = wrap(sec + 1, sections), wrap(sec - 1, sections)

    def at(a_pos, b_pos):
        z_pos = b_pos + c * (a_pos - b_pos)
        y_pos = a_pos + c * (b_pos - a_pos)
        return {"expert": (z_pos * R + y_pos) * 2 + c, "section": sec}

    a_next, a_prev = at(wrap(a + 1, R), b), at(wrap(a - 1, R), b)
    b_next, b_prev = at(a, wrap(b + 1, R)), at(a, wrap(b - 1, R))
    sibling = {"expert": chip * 2 + 1 - c, "section": sec}

    def remote(src, dst, send, recv, device):
        return pltpu.make_async_remote_copy(
            src_ref=src, dst_ref=dst, send_sem=send, recv_sem=recv, device_id=device, device_id_type=MESH
        )

    load_in = pltpu.make_async_copy(win_hbm, win, load_sem.at[0])
    load_out = pltpu.make_async_copy(wout_hbm, wout, load_sem.at[1])
    loads = [
        pltpu.make_async_copy(src, dst, load_sem.at[2 + i])
        for i, (src, dst) in enumerate(((x_hbm, x_ref), (g_hbm, g_ref), (ids_hbm, ids_ref), (aff_hbm, aff_ref)))
    ]
    for load in loads:
        load.start()
    load_in.start()
    load_out.start()

    barrier = pltpu.get_barrier_semaphore()
    source = wrap(sec - 1 + 2 * c, sections)
    peers = [a_next, a_prev, b_next, b_prev, sibling]
    peers += [{"expert": chip * 2, "section": source}, {"expert": chip * 2 + 1, "section": source}]
    if half > 1:
        peers += [at(wrap(a + 2, R), b), at(wrap(a - 2, R), b)]
    for device in peers:
        pl.semaphore_signal(barrier, inc=1, device_id=device, device_id_type=MESH)

    for load in loads:
        load.wait()

    def packed(value):
        wide = value.astype(F32)
        return jnp.concatenate([wide[:, :H], wide[:, H:]], axis=0).astype(BF16)

    shift_src[0] = packed(x_ref[...])
    shift_src[1] = packed(g_ref[...])
    chosen = aff_ref[...]
    ids = ids_ref[...]
    total = jnp.sum(chosen, axis=1, keepdims=True)
    weight = chosen / total
    lane8 = lax.broadcasted_iota(jnp.int32, (rows, LANES), 1)
    dense = jnp.zeros((rows, LANES), F32)
    for k in range(top):
        dense = dense + jnp.where(lane8 == ids[:, k : k + 1], weight[:, k : k + 1], 0.0)
    wt_src[...] = dense
    pl.semaphore_wait(barrier, len(peers))

    send_x = remote(
        shift_src.at[0], shift_dst.at[c], shift_send.at[0], shift_recv.at[c], {"expert": chip * 2, "section": sec_next}
    )
    send_g = remote(
        shift_src.at[1], shift_dst.at[c], shift_send.at[1], shift_recv.at[c], {"expert": chip * 2 + 1, "section": sec_prev}
    )
    send_w = remote(wt_src, wt_dst, wt_sem.at[0], wt_sem.at[1], sibling)
    send_x.start()
    send_g.start()
    send_w.start()
    for i in range(2):
        remote(shift_src.at[0], shift_dst.at[i], shift_send.at[0], shift_recv.at[i], sibling).wait_recv()
    send_w.wait_recv()
    low, high = shift_dst[0].astype(F32), shift_dst[1].astype(F32)
    mine, other = wt_src[...], wt_dst[...]
    pair_wt = jnp.concatenate([jnp.where(c == 0, mine, other), jnp.where(c == 0, other, mine)], axis=0)
    lead = pair_wt.astype(BF16).astype(F32)
    buf[c, b, a, :, 0:H] = jnp.concatenate([low[:rows], high[:rows]], axis=0).astype(BF16)
    buf[c, b, a, :, H:D] = jnp.concatenate([low[rows:], high[rows:]], axis=0).astype(BF16)
    buf[c, b, a, :, D:] = jnp.where(c == 0, lead, pair_wt - lead).astype(BF16)

    def along_a(j, way, hop):
        return remote(
            buf.at[c, b, j], buf.at[c, b, j], a_send.at[way, hop], a_recv.at[way, hop], a_next if way == 0 else a_prev
        )

    def along_b(origin, j, way, hop, piece):
        return remote(
            buf.at[c, origin, j],
            buf.at[c, origin, j],
            b_send.at[way, hop],
            b_recv.at[way, hop, piece],
            b_next if way == 0 else b_prev,
        )

    def to_sibling(origin, j):
        return remote(buf.at[c, origin, j], buf.at[c, origin, j], sib_send.at[origin], sib_recv.at[origin], sibling)

    def first_hop(o):
        hops, sign = order_of(R - 1 - o, R)
        j = wrap(a + sign * hops, R)

        @pl.when(o == 0)
        def _():
            if half > 1:
                along_a(j, 0, 1).start()
            along_a(j, 1, 1).start()

        @pl.when(jnp.logical_and(o > 0, sign > 0))
        def _():
            along_a(j, 1, hops).wait_recv()

            @pl.when(hops < half)
            def _():
                along_a(j, 1, hops + 1).start()

        @pl.when(jnp.logical_and(o > 0, sign < 0))
        def _():
            along_a(j, 0, hops).wait_recv()

            @pl.when(hops < half - 1)
            def _():
                along_a(j, 0, hops + 1).start()

        start_b(b, b, j, 1, o)
        to_sibling(b, j).start()

    def start_b(left, right, j, hop, o):
        even = lax.rem(o, 2) == 0
        if hop < half:
            along_b(left, j, 0, hop, o).start()
            along_b(right, j, 1, hop, o).start()
        else:

            @pl.when(even)
            def _():
                along_b(left, j, 0, hop, o).start()

            @pl.when(jnp.logical_not(even))
            def _():
                along_b(right, j, 1, hop, o).start()

    def next_hop(hop, o):
        j = place(R - 1 - o, a, R)
        left, right = wrap(b - (hop - 1), R), wrap(b + (hop - 1), R)
        if hop <= half:
            along_b(left, j, 0, hop - 1, o).wait_recv()
            along_b(right, j, 1, hop - 1, o).wait_recv()
            start_b(left, right, j, hop, o)
            to_sibling(left, j).start()
            to_sibling(right, j).start()
        else:
            even = lax.rem(o, 2) == 0

            @pl.when(even)
            def _():
                along_b(left, j, 0, half, o).wait_recv()

            @pl.when(jnp.logical_not(even))
            def _():
                along_b(left, j, 1, half, o).wait_recv()

            to_sibling(left, j).start()

    def wait_sibling(origin):
        remote(buf.at[1 - c, origin], buf.at[1 - c, origin], sib_send.at[origin], sib_recv.at[origin], sibling).wait_recv()

    def project(z_slab, y_slab):
        rows_lo = buf[0, z_slab, :, :, 0:H].reshape(R * block, H)
        rows_hi = buf[0, z_slab, :, :, H:D].reshape(R * block, H)
        ab[z_slab] = jnp.dot(rows_lo, win[0], preferred_element_type=F32) + jnp.dot(
            rows_hi, win[1], preferred_element_type=F32
        )
        rows_g = buf[1, y_slab, :, :, 0:D].reshape(R * block, D)
        q = lax.dot_general(rows_g, wout[...], (((1,), (1,)), ((), ())), preferred_element_type=F32)
        qb[:, y_slab] = q.reshape(R, block, units)

    def project_at(distance):
        def side(i, carry):
            step = distance * (1 - 2 * i)

            @pl.when(jnp.logical_or(i == 0, jnp.logical_and(distance > 0, distance < half)))
            def _():
                wait_sibling(wrap(a + step, R))
                project(wrap(z + step, R), wrap(y + step, R))

            return carry

        lax.fori_loop(0, 2, side, 0)

    def step(t, carry):
        for hop in range(1, half + 2):
            for i in range(2):
                o = 2 * (t - LAG * (hop - 1)) - 1 + i

                @pl.when(jnp.logical_and(o >= 0, o < R))
                def _():
                    if hop == 1:
                        first_hop(o)
                    else:
                        next_hop(hop, o)

        since = t - (half + 1)

        @pl.when(since == 0)
        def _():
            load_in.wait()
            load_out.wait()

        @pl.when(jnp.logical_and(since >= 0, lax.rem(since + LAG, LAG) == 0))
        def _():
            project_at(lax.div(since, LAG))

        return carry

    lax.fori_loop(0, half + LAG * half + 1, step, 0)
    project_at(half)

    def activate(z_slab, carry):
        lane = lax.broadcasted_iota(jnp.int32, (R * block, LANES), 1)
        wt = buf[0, z_slab, :, :, D:].astype(F32) + buf[1, :, z_slab, :, D:].astype(F32)
        w = jnp.sum(jnp.where(lane == expert, wt.reshape(R * block, LANES), 0.0), axis=1, keepdims=True)
        a_part = ab[z_slab, :, 0:units]
        b_part = ab[z_slab, :, units:]
        q = qb[z_slab].reshape(R * block, units) * w
        sig = jax.nn.sigmoid(a_part)
        active = a_part * sig
        hidden = active * b_part
        r = jnp.sum(hidden.astype(BF16).astype(F32) * q, axis=1, keepdims=True)
        gab[z_slab, :, :, 0:units] = (
            (q * b_part * sig * (1.0 + a_part * (1.0 - sig))).astype(BF16).reshape(R, block, units)
        )
        gab[z_slab, :, :, units:] = (q * active).astype(BF16).reshape(R, block, units)
        hw[:, z_slab] = (hidden * w).astype(BF16).reshape(R, block, units)
        rb[z_slab] = jnp.where(lane == expert, r, 0.0).astype(BF16).reshape(R, block, LANES)
        return carry

    lax.fori_loop(0, R, activate, 0)

    def spot(target, j, swap):
        return target + swap * (j - target), j + swap * (target - j)

    def products(target, centre, swap, h):
        parts = []
        for u in range(R):
            zi, yi = spot(target, place(u, centre, R), swap)
            parts.append(gab[zi, yi])
        rows_ab = jnp.concatenate(parts, axis=0)
        return lax.dot_general(rows_ab, win[h], (((1,), (1,)), ((), ())), preferred_element_type=F32)

    def pair_copy(n):
        return remote(pair_src.at[n], pair_dst.at[n], pair_send.at[n], pair_recv.at[n], sibling)

    def give(n):
        value = products(place(n, a, R), b, 1 - c, 1 - c)
        pair_src[n] = value.astype(BF16).reshape(R, block, H)
        pair_copy(n).start()

    def ring_copy(way, hop, g):
        return remote(
            ring_src.at[way, hop, g],
            ring_dst.at[way, hop, g],
            ring_send.at[way, hop],
            ring_recv.at[way, hop, g],
            b_next if way == 0 else b_prev,
        )

    def wait_ring(way, hop, g):
        ring_copy(way, hop, g).wait_recv()

    def dense_r(target, g):
        parts = []
        for i in range(per):
            zi, yi = spot(target, place(g * per + i, a, R), c)
            parts.append(rb[zi, yi].astype(F32)[None])
        return jnp.concatenate(parts, axis=0)

    def keep(n, slot):
        acc[slot] = products(place(n, b, R), a, c, c).reshape(groups, per, block, H)

    def local_sum(n, slot, g):
        value = acc[slot, g] + pair_dst[n, pl.ds(g * per, per)].astype(F32)
        return value, dense_r(place(n, b, R), g)

    def send_on(way, hop, g, value, r_value):
        ring_src[way, hop, g, :, :, 0:H] = value.astype(BF16)
        ring_src[way, hop, g, :, :, H:] = r_value.astype(BF16)

    give(0)
    keep(0, 0)
    for i in range(1, min(R, 3)):
        give(i)

    pair_copy(0).wait_recv()
    for i in range(groups // 2):
        for way in range(2):
            g = i + way * (groups // 2)
            value, r_value = local_sum(0, 0, g)
            send_on(way, half, g, value, r_value)
            ring_copy(way, half, g).start()

    def relay(partial, s, carry):
        hops = half - s
        for way in (1, 0):
            keep(2 * s - way, way)
        for way in (1, 0):
            pair_copy(2 * s - way).wait_recv()

        def group(g, carry):
            for way in (1, 0):
                n = 2 * s - way
                value, r_value = local_sum(n, way, g)

                def with_arrived():
                    wait_ring(way, hops + 1, g)
                    arrived = ring_dst[way, hops + 1, g].astype(F32)
                    send_on(way, hops, g, value + arrived[:, :, 0:H], r_value + arrived[:, :, H:])

                if partial:
                    here = lax.div(g, groups // 2) == way

                    @pl.when(here)
                    def _():
                        with_arrived()

                    @pl.when(jnp.logical_not(here))
                    def _():
                        send_on(way, hops, g, value, r_value)

                else:
                    with_arrived()
                ring_copy(way, hops, g).start()
            return carry

        lax.fori_loop(0, groups, group, 0)

        @pl.when(2 * s + 1 < R)
        def _():
            give(2 * s + 1)

        @pl.when(2 * s + 2 < R)
        def _():
            give(2 * s + 2)

        return carry

    if R > 2:
        relay(True, 1, 0)
    if R > 4:
        lax.fori_loop(2, half, functools.partial(relay, False), 0)

    def line_copy(u):
        hops, sign = order_of(u, R)
        reach = hops if hops <= 2 else hops - 2
        return remote(
            line_src.at[u], line_dst.at[u], line_send.at[u], line_recv.at[u], at(wrap(a + sign * reach, R), b)
        )

    def senders(hops, signs):
        found = []
        for u in range(R - 1):
            if order_of(u, R)[0] in hops and order_of(u, R)[1] in signs:
                found.append(u)
        return found

    chunk = D // 7 if D % (7 * LANES) == 0 else LANES
    chunks = D // chunk

    def grad_down(i):
        cols = pl.ds(pl.multiple_of(i * chunk, chunk), chunk)
        g_rows = buf[1, :, :, :, cols].reshape(R * R * block, chunk)
        h_rows = hw[...].reshape(R * R * block, units)
        gd_out[:, cols] = lax.dot_general(
            h_rows, g_rows, (((0,), (0,)), ((), ())), preferred_element_type=F32
        ).astype(BF16)

    n = R - 1
    keep(n, 0)
    pair_copy(n).wait_recv()
    done = 0
    for g in range(groups):
        value, r_value = local_sum(n, 0, g)
        for way in range(2):
            if half > 1 or (g < groups // 2) == (way == 0):
                wait_ring(way, 1, g)
                arrived = ring_dst[way, 1, g].astype(F32)
                value = value + arrived[:, :, 0:H]
                r_value = r_value + arrived[:, :, H:]
        for i in range(per):
            u = g * per + i
            hops, sign = order_of(u, R)
            v, rv = value[i], r_value[i]
            arriving = []
            if hops == 2:
                arriving = senders((3, 4), (sign,))
            elif hops == 0:
                arriving = senders((1, 2), (1, -1))
            if arriving:
                stop = chunks if hops == 0 else min(chunks, done + 2)
                while done < stop:
                    grad_down(done)
                    done += 1
            for other in arriving:
                line_copy(other).wait_recv()
                arrived = line_dst[other].astype(F32)
                v = v + arrived[:, 0:H]
                rv = rv + arrived[:, H:]
            if hops > 0:
                line_src[u, :, 0:H] = v.astype(BF16)
                line_src[u, :, H:] = rv.astype(BF16)
                line_copy(u).start()
            else:
                fin_src[:, 0:H] = jnp.where(c == 0, v[rows:], v[:rows])
                fin_src[:, H:] = jnp.where(c == 0, rv[rows:], rv[:rows])
                swap_rows = remote(fin_src, fin_dst, fin_sem.at[0], fin_sem.at[1], sibling)
                swap_rows.start()
                own_rows = jnp.where(c == 0, v[:rows], v[rows:])
                own_r = jnp.where(c == 0, rv[:rows], rv[rows:])
                swap_rows.wait_recv()
                their_rows = fin_dst[:, 0:H]
                r_all = own_r + fin_dst[:, H:]
                dx_out[:, 0:H] = jnp.where(c == 0, own_rows, their_rows).astype(BF16)
                dx_out[:, H:] = jnp.where(c == 0, their_rows, own_rows).astype(BF16)
                swap_rows.wait_send()

    column = lax.broadcasted_iota(jnp.int32, (rows, top), 1)
    r_val = jnp.zeros((rows, top), F32)
    for k in range(top):
        r_k = jnp.sum(jnp.where(lane8 == ids[:, k : k + 1], r_all, 0.0), axis=1, keepdims=True)
        r_val = r_val + jnp.where(column == k, r_k, 0.0)
    sg_out[...] = r_val / chosen - jnp.sum(r_val, axis=1, keepdims=True) / total

    send_x.wait_send()
    send_g.wait_send()
    send_w.wait_send()
    for hop in range(1, half + 1):
        if hop < half:
            along_a(a, 0, hop).wait_send()
        along_a(a, 1, hop).wait_send()
        for way in range(2):
            count = R if hop < half else half
            slab = buf.at[c, b, pl.ds(0, count)]
            remote(slab, slab, b_send.at[way, hop], b_recv.at[way, hop, 0], sibling).wait_send()
            parts = groups if hop < half else groups // 2
            sent = ring_src.at[way, hop, pl.ds(0, parts)]
            remote(sent, sent, ring_send.at[way, hop], ring_recv.at[way, hop, 0], sibling).wait_send()

    for u in range(R - 1):
        line_copy(u).wait_send()

    def settle(i, carry):
        remote(buf.at[c, i], buf.at[c, i], sib_send.at[i], sib_recv.at[i], sibling).wait_send()
        pair_copy(i).wait_send()
        return carry

    lax.fori_loop(0, R, settle, 0)


def side_of(devices):
    R = 1
    while 2 * R * R < devices:
        R += 1
    return R


def on_device(prev_out, next_grad, expert_ids, affinity, w_gate_up, w_down):
    slices = lax.axis_size("expert")
    sections = lax.axis_size("section")
    R = side_of(slices)
    rows, D = prev_out.shape[1:]
    top = expert_ids.shape[2]
    units = w_down.shape[2]
    H = D // 2
    block = 2 * rows
    split = slices // max(top, slices // 8)
    half = R // 2
    per = max(1, R // 4)
    groups = R // per
    vmem = pl.BlockSpec(memory_space=pltpu.VMEM)
    hbm = pl.BlockSpec(memory_space=pltpu.HBM)
    dma = pltpu.SemaphoreType.DMA
    flops = 2 * slices * rows * D * units * 6
    dx, gd, sg = pl.pallas_call(
        functools.partial(kernel, R, sections, split),
        out_shape=(
            jax.ShapeDtypeStruct((rows, D), BF16),
            jax.ShapeDtypeStruct((units, D), BF16),
            jax.ShapeDtypeStruct((rows, top), F32),
        ),
        in_specs=[hbm] * 6,
        out_specs=(vmem, vmem, vmem),
        scratch_shapes=[
            pltpu.VMEM((rows, D), BF16),
            pltpu.VMEM((rows, D), BF16),
            pltpu.VMEM((rows, top), jnp.int32),
            pltpu.VMEM((rows, top), F32),
            pltpu.VMEM((2, R, R, block, D + LANES), BF16),
            pltpu.VMEM((2, H, 2 * units), BF16),
            pltpu.VMEM((units, D), BF16),
            pltpu.VMEM((2, block, H), BF16),
            pltpu.VMEM((2, block, H), BF16),
            pltpu.VMEM((rows, LANES), F32),
            pltpu.VMEM((rows, LANES), F32),
            pltpu.VMEM((R, R * block, 2 * units), F32),
            pltpu.VMEM((R, R, block, units), F32),
            pltpu.VMEM((R, R, block, 2 * units), BF16),
            pltpu.VMEM((R, R, block, units), BF16),
            pltpu.VMEM((R, R, block, LANES), BF16),
            pltpu.VMEM((2, groups, per, block, H), F32),
            pltpu.VMEM((R, R, block, H), BF16),
            pltpu.VMEM((R, R, block, H), BF16),
            pltpu.VMEM((2, half + 1, groups, per, block, H + LANES), BF16),
            pltpu.VMEM((2, half + 1, groups, per, block, H + LANES), BF16),
            pltpu.VMEM((R, block, H + LANES), BF16),
            pltpu.VMEM((R, block, H + LANES), BF16),
            pltpu.VMEM((rows, H + LANES), F32),
            pltpu.VMEM((rows, H + LANES), F32),
            dma((6,)),
            dma((2,)),
            dma((2,)),
            dma((2,)),
            dma((2, half + 1)),
            dma((2, half + 1)),
            dma((2, half + 1)),
            dma((2, half + 1, R)),
            dma((R,)),
            dma((R,)),
            dma((R,)),
            dma((R,)),
            dma((2, half + 1)),
            dma((2, half + 1, groups)),
            dma((R,)),
            dma((R,)),
            dma((2,)),
        ],
        compiler_params=pltpu.CompilerParams(
            collective_id=0, has_side_effects=True, vmem_limit_bytes=VMEM_BYTES
        ),
        cost_estimate=pl.CostEstimate(flops=flops, bytes_accessed=4 * D * units * 2, transcendentals=0),
    )(
        prev_out[0],
        next_grad[0],
        expert_ids[0],
        affinity[0],
        w_gate_up[0, 0].reshape(2, H, 2 * units),
        w_down[0, 0],
    )
    return dx[None], gd[None, None], sg[None]


def solution(mesh):
    in_specs = (
        P("section", "expert", None),
        P("section", "expert", None),
        P("section", "expert", None),
        P("section", "expert", None),
        P("section", "expert", None, None),
        P("section", "expert", None, None),
    )
    out_specs = (
        P("section", "expert", None),
        P("section", "expert", None, None),
        P("section", "expert", None),
    )
    return jax.shard_map(
        on_device, mesh=mesh, in_specs=in_specs, out_specs=out_specs, check_vma=False
    )
```

```python
import functools

import jax
import jax.numpy as jnp
from jax import lax
from jax.experimental import pallas as pl
from jax.experimental.pallas import tpu as pltpu
from jax.sharding import PartitionSpec as P

MESH = pl.DeviceIdType.MESH
F32 = jnp.float32
BF16 = jnp.bfloat16
LANES = 128
LAG = 1
VMEM_BYTES = 60 * 1024 * 1024


def wrap(value, length):
    return lax.rem(value + length, length)


def order_of(index, length):
    if isinstance(index, int):
        return (length - index) // 2, 1 - 2 * (index % 2)
    return lax.div(length - index, 2), 1 - 2 * lax.rem(index, 2)


def place(index, centre, length):
    hops, sign = order_of(index, length)
    return wrap(centre + sign * hops, length)


def kernel(
    R,
    sections,
    split,
    x_hbm,
    g_hbm,
    ids_hbm,
    aff_hbm,
    win_hbm,
    wout_hbm,
    dx_out,
    gd_out,
    sg_out,
    x_ref,
    g_ref,
    ids_ref,
    aff_ref,
    buf,
    win,
    wout,
    shift_src,
    shift_dst,
    wt_src,
    wt_dst,
    ab,
    qb,
    wl,
    gab,
    hw,
    rb,
    acc,
    pair_src,
    pair_dst,
    ring_src,
    ring_dst,
    line_src,
    line_dst,
    fin_src,
    fin_dst,
    load_sem,
    shift_send,
    shift_recv,
    wt_sem,
    a_send,
    a_recv,
    b_send,
    b_recv,
    sib_send,
    sib_recv,
    pair_send,
    pair_recv,
    ring_send,
    ring_recv,
    line_send,
    line_recv,
    fin_sem,
):
    half = R // 2
    rows, D = x_ref.shape
    H = D // 2
    block = 2 * rows
    units = wout.shape[0]
    top = ids_ref.shape[1]
    per = ring_src.shape[3]
    groups = R // per
    me = lax.axis_index("expert")
    sec = lax.axis_index("section")
    c = lax.rem(me, 2)
    chip = lax.div(me, 2)
    z, y = lax.div(chip, R), lax.rem(chip, R)
    a = y + c * (z - y)
    b = z + c * (y - z)
    expert = lax.div(me, split)
    sec_next, sec_prev = wrap(sec + 1, sections), wrap(sec - 1, sections)

    def at(a_pos, b_pos):
        z_pos = b_pos + c * (a_pos - b_pos)
        y_pos = a_pos + c * (b_pos - a_pos)
        return {"expert": (z_pos * R + y_pos) * 2 + c, "section": sec}

    a_next, a_prev = at(wrap(a + 1, R), b), at(wrap(a - 1, R), b)
    b_next, b_prev = at(a, wrap(b + 1, R)), at(a, wrap(b - 1, R))
    sibling = {"expert": chip * 2 + 1 - c, "section": sec}

    def remote(src, dst, send, recv, device):
        return pltpu.make_async_remote_copy(
            src_ref=src, dst_ref=dst, send_sem=send, recv_sem=recv, device_id=device, device_id_type=MESH
        )

    load_in = pltpu.make_async_copy(win_hbm, win, load_sem.at[0])
    load_out = pltpu.make_async_copy(wout_hbm, wout, load_sem.at[1])
    loads = [
        pltpu.make_async_copy(src, dst, load_sem.at[2 + i])
        for i, (src, dst) in enumerate(((x_hbm, x_ref), (g_hbm, g_ref), (ids_hbm, ids_ref), (aff_hbm, aff_ref)))
    ]
    for load in loads:
        load.start()
    load_in.start()
    load_out.start()

    barrier = pltpu.get_barrier_semaphore()
    source = wrap(sec - 1 + 2 * c, sections)
    peers = [a_next, a_prev, b_next, b_prev, sibling]
    peers += [{"expert": chip * 2, "section": source}, {"expert": chip * 2 + 1, "section": source}]
    if half > 1:
        peers += [at(wrap(a + 2, R), b), at(wrap(a - 2, R), b)]
    for device in peers:
        pl.semaphore_signal(barrier, inc=1, device_id=device, device_id_type=MESH)

    for load in loads:
        load.wait()

    def packed(value):
        wide = value.astype(F32)
        return jnp.concatenate([wide[:, :H], wide[:, H:]], axis=0).astype(BF16)

    shift_src[0] = packed(x_ref[...])
    shift_src[1] = packed(g_ref[...])
    chosen = aff_ref[...]
    ids = ids_ref[...]
    total = jnp.sum(chosen, axis=1, keepdims=True)
    weight = chosen / total
    lane8 = lax.broadcasted_iota(jnp.int32, (rows, LANES), 1)
    dense = jnp.zeros((rows, LANES), F32)
    for k in range(top):
        dense = dense + jnp.where(lane8 == ids[:, k : k + 1], weight[:, k : k + 1], 0.0)
    wt_src[...] = dense
    pl.semaphore_wait(barrier, len(peers))

    send_x = remote(
        shift_src.at[0], shift_dst.at[c], shift_send.at[0], shift_recv.at[c], {"expert": chip * 2, "section": sec_next}
    )
    send_g = remote(
        shift_src.at[1], shift_dst.at[c], shift_send.at[1], shift_recv.at[c], {"expert": chip * 2 + 1, "section": sec_prev}
    )
    send_w = remote(wt_src, wt_dst, wt_sem.at[0], wt_sem.at[1], sibling)
    send_x.start()
    send_g.start()
    send_w.start()
    for i in range(2):
        remote(shift_src.at[0], shift_dst.at[i], shift_send.at[0], shift_recv.at[i], sibling).wait_recv()
    send_w.wait_recv()
    low, high = shift_dst[0].astype(F32), shift_dst[1].astype(F32)
    mine, other = wt_src[...], wt_dst[...]
    pair_wt = jnp.concatenate([jnp.where(c == 0, mine, other), jnp.where(c == 0, other, mine)], axis=0)
    lead = pair_wt.astype(BF16).astype(F32)
    buf[c, b, a, :, 0:H] = jnp.concatenate([low[:rows], high[:rows]], axis=0).astype(BF16)
    buf[c, b, a, :, H:D] = jnp.concatenate([low[rows:], high[rows:]], axis=0).astype(BF16)
    buf[c, b, a, :, D:] = jnp.where(c == 0, lead, pair_wt - lead).astype(BF16)

    def along_a(j, way, hop):
        return remote(
            buf.at[c, b, j], buf.at[c, b, j], a_send.at[way, hop], a_recv.at[way, hop], a_next if way == 0 else a_prev
        )

    def along_b(origin, j, way, hop, piece):
        return remote(
            buf.at[c, origin, j],
            buf.at[c, origin, j],
            b_send.at[way, hop],
            b_recv.at[way, hop, piece],
            b_next if way == 0 else b_prev,
        )

    def to_sibling(origin, j):
        return remote(buf.at[c, origin, j], buf.at[c, origin, j], sib_send.at[origin], sib_recv.at[origin], sibling)

    def first_hop(o):
        hops, sign = order_of(R - 1 - o, R)
        j = wrap(a + sign * hops, R)

        @pl.when(o == 0)
        def _():
            if half > 1:
                along_a(j, 0, 1).start()
            along_a(j, 1, 1).start()

        @pl.when(jnp.logical_and(o > 0, sign > 0))
        def _():
            along_a(j, 1, hops).wait_recv()

            @pl.when(hops < half)
            def _():
                along_a(j, 1, hops + 1).start()

        @pl.when(jnp.logical_and(o > 0, sign < 0))
        def _():
            along_a(j, 0, hops).wait_recv()

            @pl.when(hops < half - 1)
            def _():
                along_a(j, 0, hops + 1).start()

        start_b(b, b, j, 1, o)
        to_sibling(b, j).start()

    def start_b(left, right, j, hop, o):
        even = lax.rem(o, 2) == 0
        if hop < half:
            along_b(left, j, 0, hop, o).start()
            along_b(right, j, 1, hop, o).start()
        else:

            @pl.when(even)
            def _():
                along_b(left, j, 0, hop, o).start()

            @pl.when(jnp.logical_not(even))
            def _():
                along_b(right, j, 1, hop, o).start()

    def next_hop(hop, o):
        j = place(R - 1 - o, a, R)
        left, right = wrap(b - (hop - 1), R), wrap(b + (hop - 1), R)
        if hop <= half:
            along_b(left, j, 0, hop - 1, o).wait_recv()
            along_b(right, j, 1, hop - 1, o).wait_recv()
            start_b(left, right, j, hop, o)
            to_sibling(left, j).start()
            to_sibling(right, j).start()
        else:
            even = lax.rem(o, 2) == 0

            @pl.when(even)
            def _():
                along_b(left, j, 0, half, o).wait_recv()

            @pl.when(jnp.logical_not(even))
            def _():
                along_b(left, j, 1, half, o).wait_recv()

            to_sibling(left, j).start()

    def wait_sibling(origin):
        remote(buf.at[1 - c, origin], buf.at[1 - c, origin], sib_send.at[origin], sib_recv.at[origin], sibling).wait_recv()

    def project(z_slab, y_slab):
        rows_lo = buf[0, z_slab, :, :, 0:H].reshape(R * block, H)
        rows_hi = buf[0, z_slab, :, :, H:D].reshape(R * block, H)
        value = jnp.dot(rows_lo, win[0], preferred_element_type=F32) + jnp.dot(
            rows_hi, win[1], preferred_element_type=F32
        )
        ab[z_slab] = value.reshape(R, block, 2 * units)
        rows_g = buf[1, y_slab, :, :, 0:D].reshape(R * block, D)
        q = lax.dot_general(rows_g, wout[...], (((1,), (1,)), ((), ())), preferred_element_type=F32)
        qb[:, y_slab] = q.reshape(R, block, units)
        wl[:, y_slab] = buf[1, y_slab, :, :, D:]

    def project_at(distance):
        def side(i, carry):
            step = distance * (1 - 2 * i)

            @pl.when(jnp.logical_or(i == 0, jnp.logical_and(distance > 0, distance < half)))
            def _():
                wait_sibling(wrap(a + step, R))
                project(wrap(z + step, R), wrap(y + step, R))

            return carry

        lax.fori_loop(0, 2, side, 0)

    def activate(z_at, y_at):
        tall = R * block
        lane = lax.broadcasted_iota(jnp.int32, (tall, LANES), 1)
        wt = buf[0, z_at, y_at, :, D:].astype(F32) + wl[z_at, y_at].astype(F32)
        w = jnp.sum(jnp.where(lane == expert, wt.reshape(tall, LANES), 0.0), axis=1, keepdims=True)
        a_part = ab[z_at, y_at, :, 0:units].reshape(tall, units)
        b_part = ab[z_at, y_at, :, units:].reshape(tall, units)
        q = qb[z_at, y_at].reshape(tall, units) * w
        sig = jax.nn.sigmoid(a_part)
        active = a_part * sig
        hidden = active * b_part
        r = jnp.sum(hidden.astype(BF16).astype(F32) * q, axis=1, keepdims=True)
        gab[z_at, y_at, :, 0:units] = (
            (q * b_part * sig * (1.0 + a_part * (1.0 - sig))).astype(BF16).reshape(R, block, units)
        )
        gab[z_at, y_at, :, units:] = (q * active).astype(BF16).reshape(R, block, units)
        hw[y_at, z_at] = (hidden * w).astype(BF16).reshape(R, block, units)
        rb[z_at, y_at] = jnp.where(lane == expert, r, 0.0).astype(BF16).reshape(R, block, LANES)

    def forward_at(t):
        for hop in range(1, half + 2):
            for i in range(2):
                o = 2 * (t - LAG * (hop - 1)) - 1 + i

                @pl.when(jnp.logical_and(o >= 0, o < R))
                def _():
                    if hop == 1:
                        first_hop(o)
                    else:
                        next_hop(hop, o)

    def step(t, carry):
        forward_at(t)
        since = t - (half + 1)

        @pl.when(since == 0)
        def _():
            load_in.wait()
            load_out.wait()

        @pl.when(jnp.logical_and(since >= 0, lax.rem(since + LAG, LAG) == 0))
        def _():
            project_at(lax.div(since, LAG))

        return carry

    final = half + LAG * half
    lax.fori_loop(0, final, step, 0)
    if half == 1:
        load_in.wait()
        load_out.wait()
    project_at(half - 1)
    z_far, y_far = wrap(z + half, R), wrap(y + half, R)
    qb[:, y_far] = jnp.zeros((R, block, units), F32)
    wl[:, y_far] = jnp.zeros((R, block, LANES), BF16)

    def near(i, carry):
        activate(wrap(z_far + 1 + i, R), slice(None))
        return carry

    lax.fori_loop(0, R - 1, near, 0)
    forward_at(final)
    project_at(half)
    activate(z_far, slice(None))
    activate(slice(None), y_far)


    def spot(target, j, swap):
        return target + swap * (j - target), j + swap * (target - j)

    def products(target, centre, swap, h):
        parts = []
        for u in range(R):
            zi, yi = spot(target, place(u, centre, R), swap)
            parts.append(gab[zi, yi])
        rows_ab = jnp.concatenate(parts, axis=0)
        return lax.dot_general(rows_ab, win[h], (((1,), (1,)), ((), ())), preferred_element_type=F32)

    def pair_copy(n):
        return remote(pair_src.at[n], pair_dst.at[n], pair_send.at[n], pair_recv.at[n], sibling)

    def give(n):
        value = products(place(n, a, R), b, 1 - c, 1 - c)
        pair_src[n] = value.astype(BF16).reshape(R, block, H)
        pair_copy(n).start()

    def ring_copy(way, hop, g):
        return remote(
            ring_src.at[way, hop, g],
            ring_dst.at[way, hop, g],
            ring_send.at[way, hop],
            ring_recv.at[way, hop, g],
            b_next if way == 0 else b_prev,
        )

    def wait_ring(way, hop, g):
        ring_copy(way, hop, g).wait_recv()

    def dense_r(target, g):
        parts = []
        for i in range(per):
            zi, yi = spot(target, place(g * per + i, a, R), c)
            parts.append(rb[zi, yi].astype(F32)[None])
        return jnp.concatenate(parts, axis=0)

    def keep(n, slot):
        acc[slot] = products(place(n, b, R), a, c, c).reshape(groups, per, block, H)

    def local_sum(n, slot, g):
        value = acc[slot, g] + pair_dst[n, pl.ds(g * per, per)].astype(F32)
        return value, dense_r(place(n, b, R), g)

    def send_on(way, hop, g, value, r_value):
        ring_src[way, hop, g, :, :, 0:H] = value.astype(BF16)
        ring_src[way, hop, g, :, :, H:] = r_value.astype(BF16)

    give(0)
    keep(0, 0)
    give(1)

    pair_copy(0).wait_recv()
    for i in range(groups // 2):
        for way in range(2):
            g = i + way * (groups // 2)
            value, r_value = local_sum(0, 0, g)
            send_on(way, half, g, value, r_value)
            ring_copy(way, half, g).start()
    if R > 2:
        give(2)

    def relay(partial, s, carry):
        hops = half - s
        for way in (1, 0):
            keep(2 * s - way, way)
        for way in (1, 0):
            pair_copy(2 * s - way).wait_recv()

        def group(g, carry):
            for way in (1, 0):
                n = 2 * s - way
                value, r_value = local_sum(n, way, g)

                def with_arrived():
                    wait_ring(way, hops + 1, g)
                    arrived = ring_dst[way, hops + 1, g].astype(F32)
                    send_on(way, hops, g, value + arrived[:, :, 0:H], r_value + arrived[:, :, H:])

                if partial:
                    here = lax.div(g, groups // 2) == way

                    @pl.when(here)
                    def _():
                        with_arrived()

                    @pl.when(jnp.logical_not(here))
                    def _():
                        send_on(way, hops, g, value, r_value)

                else:
                    with_arrived()
                ring_copy(way, hops, g).start()
            return carry

        lax.fori_loop(0, groups, group, 0)

        @pl.when(2 * s + 1 < R)
        def _():
            give(2 * s + 1)

        @pl.when(2 * s + 2 < R)
        def _():
            give(2 * s + 2)

        return carry

    if R > 2:
        relay(True, 1, 0)
    if R > 4:
        lax.fori_loop(2, half, functools.partial(relay, False), 0)

    def line_copy(u):
        hops, sign = order_of(u, R)
        reach = hops if hops <= 2 else hops - 2
        return remote(
            line_src.at[u], line_dst.at[u], line_send.at[u], line_recv.at[u], at(wrap(a + sign * reach, R), b)
        )

    def senders(hops, signs):
        found = []
        for u in range(R - 1):
            if order_of(u, R)[0] in hops and order_of(u, R)[1] in signs:
                found.append(u)
        return found

    chunk = D // 7 if D % (7 * LANES) == 0 else LANES
    chunks = D // chunk

    def grad_down(i):
        cols = pl.ds(pl.multiple_of(i * chunk, chunk), chunk)
        g_rows = buf[1, :, :, :, cols].reshape(R * R * block, chunk)
        h_rows = hw[...].reshape(R * R * block, units)
        gd_out[:, cols] = lax.dot_general(
            h_rows, g_rows, (((0,), (0,)), ((), ())), preferred_element_type=F32
        ).astype(BF16)

    n = R - 1
    keep(n, 0)
    pair_copy(n).wait_recv()
    done = 0
    for g in range(groups):
        value, r_value = local_sum(n, 0, g)
        for way in range(2):
            if half > 1 or (g < groups // 2) == (way == 0):
                wait_ring(way, 1, g)
                arrived = ring_dst[way, 1, g].astype(F32)
                value = value + arrived[:, :, 0:H]
                r_value = r_value + arrived[:, :, H:]
        for i in range(per):
            u = g * per + i
            hops, sign = order_of(u, R)
            v, rv = value[i], r_value[i]
            arriving = []
            if hops == 2:
                arriving = senders((3, 4), (sign,))
            elif hops == 0:
                arriving = senders((1, 2), (1, -1))
            if arriving:
                stop = chunks if hops == 0 else min(chunks, done + 2)
                while done < stop:
                    grad_down(done)
                    done += 1
            for other in arriving:
                line_copy(other).wait_recv()
                arrived = line_dst[other].astype(F32)
                v = v + arrived[:, 0:H]
                rv = rv + arrived[:, H:]
            if hops > 0:
                line_src[u, :, 0:H] = v.astype(BF16)
                line_src[u, :, H:] = rv.astype(BF16)
                line_copy(u).start()
            else:
                fin_src[:, 0:H] = jnp.where(c == 0, v[rows:], v[:rows])
                fin_src[:, H:] = jnp.where(c == 0, rv[rows:], rv[:rows])
                swap_rows = remote(fin_src, fin_dst, fin_sem.at[0], fin_sem.at[1], sibling)
                swap_rows.start()
                own_rows = jnp.where(c == 0, v[:rows], v[rows:])
                own_r = jnp.where(c == 0, rv[:rows], rv[rows:])
                swap_rows.wait_recv()
                their_rows = fin_dst[:, 0:H]
                r_all = own_r + fin_dst[:, H:]
                dx_out[:, 0:H] = jnp.where(c == 0, own_rows, their_rows).astype(BF16)
                dx_out[:, H:] = jnp.where(c == 0, their_rows, own_rows).astype(BF16)
                swap_rows.wait_send()

    column = lax.broadcasted_iota(jnp.int32, (rows, top), 1)
    r_val = jnp.zeros((rows, top), F32)
    for k in range(top):
        r_k = jnp.sum(jnp.where(lane8 == ids[:, k : k + 1], r_all, 0.0), axis=1, keepdims=True)
        r_val = r_val + jnp.where(column == k, r_k, 0.0)
    sg_out[...] = r_val / chosen - jnp.sum(r_val, axis=1, keepdims=True) / total

    send_x.wait_send()
    send_g.wait_send()
    send_w.wait_send()
    for hop in range(1, half + 1):
        if hop < half:
            along_a(a, 0, hop).wait_send()
        along_a(a, 1, hop).wait_send()
        for way in range(2):
            count = R if hop < half else half
            slab = buf.at[c, b, pl.ds(0, count)]
            remote(slab, slab, b_send.at[way, hop], b_recv.at[way, hop, 0], sibling).wait_send()
            parts = groups if hop < half else groups // 2
            sent = ring_src.at[way, hop, pl.ds(0, parts)]
            remote(sent, sent, ring_send.at[way, hop], ring_recv.at[way, hop, 0], sibling).wait_send()

    for u in range(R - 1):
        line_copy(u).wait_send()

    def settle(i, carry):
        remote(buf.at[c, i], buf.at[c, i], sib_send.at[i], sib_recv.at[i], sibling).wait_send()
        pair_copy(i).wait_send()
        return carry

    lax.fori_loop(0, R, settle, 0)


def finish(dx_in, gd_in, sg_in, dx_out, gd_out, sg_out, dx_mid, gd_mid, sg_mid, sem):
    into = ((dx_in, dx_mid), (gd_in, gd_mid), (sg_in, sg_mid))
    out = ((dx_mid, dx_out), (gd_mid, gd_out), (sg_mid, sg_out))
    loads = [pltpu.make_async_copy(src, dst, sem.at[0, i]) for i, (src, dst) in enumerate(into)]
    stores = [pltpu.make_async_copy(src, dst, sem.at[1, i]) for i, (src, dst) in enumerate(out)]
    for load in loads:
        load.start()
    for load, store in zip(loads, stores):
        load.wait()
        store.start()
    for store in stores:
        store.wait()


def side_of(devices):
    R = 1
    while 2 * R * R < devices:
        R += 1
    return R


def on_device(prev_out, next_grad, expert_ids, affinity, w_gate_up, w_down):
    slices = lax.axis_size("expert")
    sections = lax.axis_size("section")
    R = side_of(slices)
    rows, D = prev_out.shape[1:]
    top = expert_ids.shape[2]
    units = w_down.shape[2]
    H = D // 2
    block = 2 * rows
    split = slices // max(top, slices // 8)
    half = R // 2
    per = max(1, R // 4)
    groups = R // per
    vmem = pl.BlockSpec(memory_space=pltpu.VMEM)
    hbm = pl.BlockSpec(memory_space=pltpu.HBM)
    dma = pltpu.SemaphoreType.DMA
    flops = 2 * slices * rows * D * units * 6
    dx, gd, sg = pl.pallas_call(
        functools.partial(kernel, R, sections, split),
        out_shape=(
            jax.ShapeDtypeStruct((rows, D), BF16),
            jax.ShapeDtypeStruct((units, D), BF16),
            jax.ShapeDtypeStruct((rows, top), F32),
        ),
        in_specs=[hbm] * 6,
        out_specs=(vmem, vmem, vmem),
        scratch_shapes=[
            pltpu.VMEM((rows, D), BF16),
            pltpu.VMEM((rows, D), BF16),
            pltpu.VMEM((rows, top), jnp.int32),
            pltpu.VMEM((rows, top), F32),
            pltpu.VMEM((2, R, R, block, D + LANES), BF16),
            pltpu.VMEM((2, H, 2 * units), BF16),
            pltpu.VMEM((units, D), BF16),
            pltpu.VMEM((2, block, H), BF16),
            pltpu.VMEM((2, block, H), BF16),
            pltpu.VMEM((rows, LANES), F32),
            pltpu.VMEM((rows, LANES), F32),
            pltpu.VMEM((R, R, block, 2 * units), F32),
            pltpu.VMEM((R, R, block, units), F32),
            pltpu.VMEM((R, R, block, LANES), BF16),
            pltpu.VMEM((R, R, block, 2 * units), BF16),
            pltpu.VMEM((R, R, block, units), BF16),
            pltpu.VMEM((R, R, block, LANES), BF16),
            pltpu.VMEM((2, groups, per, block, H), F32),
            pltpu.VMEM((R, R, block, H), BF16),
            pltpu.VMEM((R, R, block, H), BF16),
            pltpu.VMEM((2, half + 1, groups, per, block, H + LANES), BF16),
            pltpu.VMEM((2, half + 1, groups, per, block, H + LANES), BF16),
            pltpu.VMEM((R, block, H + LANES), BF16),
            pltpu.VMEM((R, block, H + LANES), BF16),
            pltpu.VMEM((rows, H + LANES), F32),
            pltpu.VMEM((rows, H + LANES), F32),
            dma((6,)),
            dma((2,)),
            dma((2,)),
            dma((2,)),
            dma((2, half + 1)),
            dma((2, half + 1)),
            dma((2, half + 1)),
            dma((2, half + 1, R)),
            dma((R,)),
            dma((R,)),
            dma((R,)),
            dma((R,)),
            dma((2, half + 1)),
            dma((2, half + 1, groups)),
            dma((R,)),
            dma((R,)),
            dma((2,)),
        ],
        compiler_params=pltpu.CompilerParams(
            collective_id=0, has_side_effects=True, vmem_limit_bytes=VMEM_BYTES
        ),
        cost_estimate=pl.CostEstimate(flops=flops, bytes_accessed=4 * D * units * 2, transcendentals=0),
    )(
        prev_out[0],
        next_grad[0],
        expert_ids[0],
        affinity[0],
        w_gate_up[0, 0].reshape(2, H, 2 * units),
        w_down[0, 0],
    )
    dx, gd, sg = pl.pallas_call(
        finish,
        out_shape=(
            jax.ShapeDtypeStruct((rows, D), BF16),
            jax.ShapeDtypeStruct((units, D), BF16),
            jax.ShapeDtypeStruct((rows, top), F32),
        ),
        in_specs=[hbm] * 3,
        out_specs=(hbm,) * 3,
        scratch_shapes=[pltpu.VMEM((rows, D), BF16), pltpu.VMEM((units, D), BF16), pltpu.VMEM((rows, top), F32), dma((2, 3))],
        compiler_params=pltpu.CompilerParams(vmem_limit_bytes=VMEM_BYTES),
        cost_estimate=pl.CostEstimate(flops=0, bytes_accessed=4 * D * (units + rows), transcendentals=0),
    )(dx, gd, sg)
    return dx[None], gd[None, None], sg[None]


def solution(mesh):
    in_specs = (
        P("section", "expert", None),
        P("section", "expert", None),
        P("section", "expert", None),
        P("section", "expert", None),
        P("section", "expert", None, None),
        P("section", "expert", None, None),
    )
    out_specs = (
        P("section", "expert", None),
        P("section", "expert", None, None),
        P("section", "expert", None),
    )
    return jax.shard_map(
        on_device, mesh=mesh, in_specs=in_specs, out_specs=out_specs, check_vma=False
    )
```

```python
import functools

import jax
import jax.numpy as jnp
from jax import lax
from jax.experimental import pallas as pl
from jax.experimental.pallas import tpu as pltpu
from jax.sharding import PartitionSpec as P

MESH = pl.DeviceIdType.MESH
F32 = jnp.float32
BF16 = jnp.bfloat16
LANES = 128
LAG = 1
VMEM_BYTES = 60 * 1024 * 1024


def wrap(value, length):
    return lax.rem(value + length, length)


def order_of(index, length):
    if isinstance(index, int):
        return (length - index) // 2, 1 - 2 * (index % 2)
    return lax.div(length - index, 2), 1 - 2 * lax.rem(index, 2)


def place(index, centre, length):
    hops, sign = order_of(index, length)
    return wrap(centre + sign * hops, length)


def kernel(
    R,
    sections,
    split,
    x_hbm,
    g_hbm,
    ids_hbm,
    aff_hbm,
    win_hbm,
    wout_hbm,
    dx_out,
    gd_out,
    sg_out,
    x_ref,
    g_ref,
    ids_ref,
    aff_ref,
    buf,
    win,
    wout,
    shift_src,
    shift_dst,
    wt_src,
    wt_dst,
    ab,
    qb,
    wl,
    gab,
    hw,
    rb,
    acc,
    pair_src,
    pair_dst,
    ring_src,
    ring_dst,
    line_src,
    line_dst,
    fin_src,
    fin_dst,
    load_sem,
    shift_send,
    shift_recv,
    wt_sem,
    a_send,
    a_recv,
    b_send,
    b_recv,
    sib_send,
    sib_recv,
    pair_send,
    pair_recv,
    ring_send,
    ring_recv,
    line_send,
    line_recv,
    fin_sem,
):
    half = R // 2
    rows, D = x_ref.shape
    H = D // 2
    block = 2 * rows
    units = wout.shape[0]
    top = ids_ref.shape[1]
    per = ring_src.shape[3]
    groups = R // per
    me = lax.axis_index("expert")
    sec = lax.axis_index("section")
    c = lax.rem(me, 2)
    chip = lax.div(me, 2)
    z, y = lax.div(chip, R), lax.rem(chip, R)
    a = y + c * (z - y)
    b = z + c * (y - z)
    expert = lax.div(me, split)
    sec_next, sec_prev = wrap(sec + 1, sections), wrap(sec - 1, sections)

    def at(a_pos, b_pos):
        z_pos = b_pos + c * (a_pos - b_pos)
        y_pos = a_pos + c * (b_pos - a_pos)
        return {"expert": (z_pos * R + y_pos) * 2 + c, "section": sec}

    a_next, a_prev = at(wrap(a + 1, R), b), at(wrap(a - 1, R), b)
    b_next, b_prev = at(a, wrap(b + 1, R)), at(a, wrap(b - 1, R))
    sibling = {"expert": chip * 2 + 1 - c, "section": sec}

    def remote(src, dst, send, recv, device):
        return pltpu.make_async_remote_copy(
            src_ref=src, dst_ref=dst, send_sem=send, recv_sem=recv, device_id=device, device_id_type=MESH
        )

    load_in = pltpu.make_async_copy(win_hbm, win, load_sem.at[0])
    load_out = pltpu.make_async_copy(wout_hbm, wout, load_sem.at[1])
    loads = [
        pltpu.make_async_copy(src, dst, load_sem.at[2 + i])
        for i, (src, dst) in enumerate(((x_hbm, x_ref), (g_hbm, g_ref), (ids_hbm, ids_ref), (aff_hbm, aff_ref)))
    ]
    for load in loads:
        load.start()
    load_in.start()
    load_out.start()

    barrier = pltpu.get_barrier_semaphore()
    source = wrap(sec - 1 + 2 * c, sections)
    peers = [a_next, a_prev, b_next, b_prev, sibling]
    peers += [{"expert": chip * 2, "section": source}, {"expert": chip * 2 + 1, "section": source}]
    if half > 1:
        peers += [at(wrap(a + 2, R), b), at(wrap(a - 2, R), b)]
    for device in peers:
        pl.semaphore_signal(barrier, inc=1, device_id=device, device_id_type=MESH)

    for load in loads:
        load.wait()

    def packed(value):
        wide = value.astype(F32)
        return jnp.concatenate([wide[:, :H], wide[:, H:]], axis=0).astype(BF16)

    shift_src[0] = packed(x_ref[...])
    shift_src[1] = packed(g_ref[...])
    chosen = aff_ref[...]
    ids = ids_ref[...]
    total = jnp.sum(chosen, axis=1, keepdims=True)
    weight = chosen / total
    lane8 = lax.broadcasted_iota(jnp.int32, (rows, LANES), 1)
    dense = jnp.zeros((rows, LANES), F32)
    for k in range(top):
        dense = dense + jnp.where(lane8 == ids[:, k : k + 1], weight[:, k : k + 1], 0.0)
    wt_src[...] = dense
    pl.semaphore_wait(barrier, len(peers))

    send_x = remote(
        shift_src.at[0], shift_dst.at[c], shift_send.at[0], shift_recv.at[c], {"expert": chip * 2, "section": sec_next}
    )
    send_g = remote(
        shift_src.at[1], shift_dst.at[c], shift_send.at[1], shift_recv.at[c], {"expert": chip * 2 + 1, "section": sec_prev}
    )
    send_w = remote(wt_src, wt_dst, wt_sem.at[0], wt_sem.at[1], sibling)
    send_x.start()
    send_g.start()
    send_w.start()
    for i in range(2):
        remote(shift_src.at[0], shift_dst.at[i], shift_send.at[0], shift_recv.at[i], sibling).wait_recv()
    send_w.wait_recv()
    low, high = shift_dst[0].astype(F32), shift_dst[1].astype(F32)
    mine, other = wt_src[...], wt_dst[...]
    pair_wt = jnp.concatenate([jnp.where(c == 0, mine, other), jnp.where(c == 0, other, mine)], axis=0)
    lead = pair_wt.astype(BF16).astype(F32)
    buf[c, b, a, :, 0:H] = jnp.concatenate([low[:rows], high[:rows]], axis=0).astype(BF16)
    buf[c, b, a, :, H:D] = jnp.concatenate([low[rows:], high[rows:]], axis=0).astype(BF16)
    buf[c, b, a, :, D:] = jnp.where(c == 0, lead, pair_wt - lead).astype(BF16)

    def along_a(j, way, hop, reach=1):
        device = at(wrap(a + (reach if way == 0 else -reach), R), b)
        return remote(buf.at[c, b, j], buf.at[c, b, j], a_send.at[way, hop], a_recv.at[way, hop], device)

    def start_a(j, base):
        for reach in (1, 2):
            for way in range(2):
                if base + reach <= (half - 1 if way == 0 else half):
                    along_a(j, way, base + reach, reach).start()

    def along_b(origin, j, way, hop, piece):
        return remote(
            buf.at[c, origin, j],
            buf.at[c, origin, j],
            b_send.at[way, hop],
            b_recv.at[way, hop, piece],
            b_next if way == 0 else b_prev,
        )

    def to_sibling(origin, j):
        return remote(buf.at[c, origin, j], buf.at[c, origin, j], sib_send.at[origin], sib_recv.at[origin], sibling)

    def relay_a(j, way, hops):
        @pl.when(hops == 2)
        def _():
            for reach in (1, 2):
                if 2 + reach <= (half - 1 if way == 0 else half):
                    along_a(j, way, 2 + reach, reach).start()

    def first_hop(o):
        hops, sign = order_of(R - 1 - o, R)
        j = wrap(a + sign * hops, R)

        @pl.when(o == 0)
        def _():
            start_a(j, 0)

        @pl.when(jnp.logical_and(o > 0, sign > 0))
        def _():
            along_a(j, 1, hops).wait_recv()
            relay_a(j, 1, hops)

        @pl.when(jnp.logical_and(o > 0, sign < 0))
        def _():
            along_a(j, 0, hops).wait_recv()
            relay_a(j, 0, hops)

        start_b(b, b, j, 1, o)
        to_sibling(b, j).start()

    def start_b(left, right, j, hop, o):
        even = lax.rem(o, 2) == 0
        if hop < half:
            along_b(left, j, 0, hop, o).start()
            along_b(right, j, 1, hop, o).start()
        else:

            @pl.when(even)
            def _():
                along_b(left, j, 0, hop, o).start()

            @pl.when(jnp.logical_not(even))
            def _():
                along_b(right, j, 1, hop, o).start()

    def next_hop(hop, o):
        j = place(R - 1 - o, a, R)
        left, right = wrap(b - (hop - 1), R), wrap(b + (hop - 1), R)
        if hop <= half:
            along_b(left, j, 0, hop - 1, o).wait_recv()
            along_b(right, j, 1, hop - 1, o).wait_recv()
            start_b(left, right, j, hop, o)
            to_sibling(left, j).start()
            to_sibling(right, j).start()
        else:
            even = lax.rem(o, 2) == 0

            @pl.when(even)
            def _():
                along_b(left, j, 0, half, o).wait_recv()

            @pl.when(jnp.logical_not(even))
            def _():
                along_b(left, j, 1, half, o).wait_recv()

            to_sibling(left, j).start()

    def wait_sibling(origin):
        remote(buf.at[1 - c, origin], buf.at[1 - c, origin], sib_send.at[origin], sib_recv.at[origin], sibling).wait_recv()

    def project(z_slab, y_slab):
        rows_lo = buf[0, z_slab, :, :, 0:H].reshape(R * block, H)
        rows_hi = buf[0, z_slab, :, :, H:D].reshape(R * block, H)
        value = jnp.dot(rows_lo, win[0], preferred_element_type=F32) + jnp.dot(
            rows_hi, win[1], preferred_element_type=F32
        )
        ab[z_slab] = value.reshape(R, block, 2 * units)
        rows_g = buf[1, y_slab, :, :, 0:D].reshape(R * block, D)
        q = lax.dot_general(rows_g, wout[...], (((1,), (1,)), ((), ())), preferred_element_type=F32)
        qb[:, y_slab] = q.reshape(R, block, units)
        wl[:, y_slab] = buf[1, y_slab, :, :, D:]

    def project_at(distance):
        def side(i, carry):
            step = distance * (1 - 2 * i)

            @pl.when(jnp.logical_or(i == 0, jnp.logical_and(distance > 0, distance < half)))
            def _():
                wait_sibling(wrap(a + step, R))
                project(wrap(z + step, R), wrap(y + step, R))

            return carry

        lax.fori_loop(0, 2, side, 0)

    def activate(z_at, y_at):
        tall = R * block
        lane = lax.broadcasted_iota(jnp.int32, (tall, LANES), 1)
        wt = buf[0, z_at, y_at, :, D:].astype(F32) + wl[z_at, y_at].astype(F32)
        w = jnp.sum(jnp.where(lane == expert, wt.reshape(tall, LANES), 0.0), axis=1, keepdims=True)
        a_part = ab[z_at, y_at, :, 0:units].reshape(tall, units)
        b_part = ab[z_at, y_at, :, units:].reshape(tall, units)
        q = qb[z_at, y_at].reshape(tall, units) * w
        sig = jax.nn.sigmoid(a_part)
        active = a_part * sig
        hidden = active * b_part
        r = jnp.sum(hidden.astype(BF16).astype(F32) * q, axis=1, keepdims=True)
        gab[z_at, y_at, :, 0:units] = (
            (q * b_part * sig * (1.0 + a_part * (1.0 - sig))).astype(BF16).reshape(R, block, units)
        )
        gab[z_at, y_at, :, units:] = (q * active).astype(BF16).reshape(R, block, units)
        hw[y_at, z_at] = (hidden * w).astype(BF16).reshape(R, block, units)
        rb[z_at, y_at] = jnp.where(lane == expert, r, 0.0).astype(BF16).reshape(R, block, LANES)

    def forward_at(t):
        for hop in range(1, half + 2):
            for i in range(2):
                o = 2 * (t - LAG * (hop - 1)) - 1 + i

                @pl.when(jnp.logical_and(o >= 0, o < R))
                def _():
                    if hop == 1:
                        first_hop(o)
                    else:
                        next_hop(hop, o)

    def step(t, carry):
        forward_at(t)
        since = t - (half + 1)

        @pl.when(since == 0)
        def _():
            load_in.wait()
            load_out.wait()

        @pl.when(jnp.logical_and(since >= 0, lax.rem(since + LAG, LAG) == 0))
        def _():
            project_at(lax.div(since, LAG))

        return carry

    final = half + LAG * half
    lax.fori_loop(0, final, step, 0)
    if half == 1:
        load_in.wait()
        load_out.wait()
    project_at(half - 1)
    z_far, y_far = wrap(z + half, R), wrap(y + half, R)
    qb[:, y_far] = jnp.zeros((R, block, units), F32)
    wl[:, y_far] = jnp.zeros((R, block, LANES), BF16)

    def near(i, carry):
        activate(wrap(z_far + 1 + i, R), slice(None))
        return carry

    lax.fori_loop(0, R - 1, near, 0)
    forward_at(final)
    project_at(half)
    activate(z_far, slice(None))
    activate(slice(None), y_far)


    def spot(target, j, swap):
        return target + swap * (j - target), j + swap * (target - j)

    def products(target, centre, swap, h):
        parts = []
        for u in range(R):
            zi, yi = spot(target, place(u, centre, R), swap)
            parts.append(gab[zi, yi])
        rows_ab = jnp.concatenate(parts, axis=0)
        return lax.dot_general(rows_ab, win[h], (((1,), (1,)), ((), ())), preferred_element_type=F32)

    def pair_copy(n):
        return remote(pair_src.at[n], pair_dst.at[n], pair_send.at[n], pair_recv.at[n], sibling)

    def give(n):
        value = products(place(n, a, R), b, 1 - c, 1 - c)
        pair_src[n] = value.astype(BF16).reshape(R, block, H)
        pair_copy(n).start()

    def ring_copy(way, hop, g):
        return remote(
            ring_src.at[way, hop, g],
            ring_dst.at[way, hop, g],
            ring_send.at[way, hop],
            ring_recv.at[way, hop, g],
            b_next if way == 0 else b_prev,
        )

    def wait_ring(way, hop, g):
        ring_copy(way, hop, g).wait_recv()

    def dense_r(target, g):
        parts = []
        for i in range(per):
            zi, yi = spot(target, place(g * per + i, a, R), c)
            parts.append(rb[zi, yi].astype(F32)[None])
        return jnp.concatenate(parts, axis=0)

    def keep(n, slot):
        acc[slot] = products(place(n, b, R), a, c, c).reshape(groups, per, block, H)

    def local_sum(n, slot, g):
        value = acc[slot, g] + pair_dst[n, pl.ds(g * per, per)].astype(F32)
        return value, dense_r(place(n, b, R), g)

    def send_on(way, hop, g, value, r_value):
        ring_src[way, hop, g, :, :, 0:H] = value.astype(BF16)
        ring_src[way, hop, g, :, :, H:] = r_value.astype(BF16)

    give(0)
    keep(0, 0)
    give(1)

    pair_copy(0).wait_recv()
    for i in range(groups // 2):
        for way in range(2):
            g = i + way * (groups // 2)
            value, r_value = local_sum(0, 0, g)
            send_on(way, half, g, value, r_value)
            ring_copy(way, half, g).start()
    if R > 2:
        give(2)

    def relay(partial, s, carry):
        hops = half - s
        for way in (1, 0):
            keep(2 * s - way, way)
        for way in (1, 0):
            pair_copy(2 * s - way).wait_recv()

        def group(g, carry):
            for way in (1, 0):
                n = 2 * s - way
                value, r_value = local_sum(n, way, g)

                def with_arrived():
                    wait_ring(way, hops + 1, g)
                    arrived = ring_dst[way, hops + 1, g].astype(F32)
                    send_on(way, hops, g, value + arrived[:, :, 0:H], r_value + arrived[:, :, H:])

                if partial:
                    here = lax.div(g, groups // 2) == way

                    @pl.when(here)
                    def _():
                        with_arrived()

                    @pl.when(jnp.logical_not(here))
                    def _():
                        send_on(way, hops, g, value, r_value)

                else:
                    with_arrived()
                ring_copy(way, hops, g).start()
            return carry

        lax.fori_loop(0, groups, group, 0)

        @pl.when(2 * s + 1 < R)
        def _():
            give(2 * s + 1)

        @pl.when(2 * s + 2 < R)
        def _():
            give(2 * s + 2)

        return carry

    if R > 2:
        relay(True, 1, 0)
    if R > 4:
        lax.fori_loop(2, half, functools.partial(relay, False), 0)

    def line_copy(u):
        hops, sign = order_of(u, R)
        reach = hops if hops <= 2 else hops - 2
        return remote(
            line_src.at[u], line_dst.at[u], line_send.at[u], line_recv.at[u], at(wrap(a + sign * reach, R), b)
        )

    def senders(hops, signs):
        found = []
        for u in range(R - 1):
            if order_of(u, R)[0] in hops and order_of(u, R)[1] in signs:
                found.append(u)
        return found

    chunk = D // 7 if D % (7 * LANES) == 0 else LANES
    chunks = D // chunk

    def grad_down(i):
        cols = pl.ds(pl.multiple_of(i * chunk, chunk), chunk)
        g_rows = buf[1, :, :, :, cols].reshape(R * R * block, chunk)
        h_rows = hw[...].reshape(R * R * block, units)
        gd_out[:, cols] = lax.dot_general(
            h_rows, g_rows, (((0,), (0,)), ((), ())), preferred_element_type=F32
        ).astype(BF16)

    n = R - 1
    keep(n, 0)
    pair_copy(n).wait_recv()
    done = 0
    for g in range(groups):
        value, r_value = local_sum(n, 0, g)
        for way in range(2):
            if half > 1 or (g < groups // 2) == (way == 0):
                wait_ring(way, 1, g)
                arrived = ring_dst[way, 1, g].astype(F32)
                value = value + arrived[:, :, 0:H]
                r_value = r_value + arrived[:, :, H:]
        for i in range(per):
            u = g * per + i
            hops, sign = order_of(u, R)
            v, rv = value[i], r_value[i]
            arriving = []
            if hops == 2:
                arriving = senders((3, 4), (sign,))
            elif hops == 0:
                arriving = senders((1, 2), (1, -1))
            if arriving:
                stop = chunks if hops == 0 else min(chunks, done + 2)
                while done < stop:
                    grad_down(done)
                    done += 1
            for other in arriving:
                line_copy(other).wait_recv()
                arrived = line_dst[other].astype(F32)
                v = v + arrived[:, 0:H]
                rv = rv + arrived[:, H:]
            if hops > 0:
                line_src[u, :, 0:H] = v.astype(BF16)
                line_src[u, :, H:] = rv.astype(BF16)
                line_copy(u).start()
            else:
                fin_src[:, 0:H] = jnp.where(c == 0, v[rows:], v[:rows])
                fin_src[:, H:] = jnp.where(c == 0, rv[rows:], rv[:rows])
                swap_rows = remote(fin_src, fin_dst, fin_sem.at[0], fin_sem.at[1], sibling)
                swap_rows.start()
                own_rows = jnp.where(c == 0, v[:rows], v[rows:])
                own_r = jnp.where(c == 0, rv[:rows], rv[rows:])
                swap_rows.wait_recv()
                their_rows = fin_dst[:, 0:H]
                r_all = own_r + fin_dst[:, H:]
                dx_out[:, 0:H] = jnp.where(c == 0, own_rows, their_rows).astype(BF16)
                dx_out[:, H:] = jnp.where(c == 0, their_rows, own_rows).astype(BF16)
                swap_rows.wait_send()

    column = lax.broadcasted_iota(jnp.int32, (rows, top), 1)
    r_val = jnp.zeros((rows, top), F32)
    for k in range(top):
        r_k = jnp.sum(jnp.where(lane8 == ids[:, k : k + 1], r_all, 0.0), axis=1, keepdims=True)
        r_val = r_val + jnp.where(column == k, r_k, 0.0)
    sg_out[...] = r_val / chosen - jnp.sum(r_val, axis=1, keepdims=True) / total

    send_x.wait_send()
    send_g.wait_send()
    send_w.wait_send()
    for hop in range(1, half + 1):
        if hop < half:
            along_a(a, 0, hop).wait_send()
        along_a(a, 1, hop).wait_send()
        for way in range(2):
            count = R if hop < half else half
            slab = buf.at[c, b, pl.ds(0, count)]
            remote(slab, slab, b_send.at[way, hop], b_recv.at[way, hop, 0], sibling).wait_send()
            parts = groups if hop < half else groups // 2
            sent = ring_src.at[way, hop, pl.ds(0, parts)]
            remote(sent, sent, ring_send.at[way, hop], ring_recv.at[way, hop, 0], sibling).wait_send()

    for u in range(R - 1):
        line_copy(u).wait_send()

    def settle(i, carry):
        remote(buf.at[c, i], buf.at[c, i], sib_send.at[i], sib_recv.at[i], sibling).wait_send()
        pair_copy(i).wait_send()
        return carry

    lax.fori_loop(0, R, settle, 0)


def finish(dx_in, gd_in, sg_in, dx_out, gd_out, sg_out, dx_mid, gd_mid, sg_mid, sem):
    into = ((dx_in, dx_mid), (gd_in, gd_mid), (sg_in, sg_mid))
    out = ((dx_mid, dx_out), (gd_mid, gd_out), (sg_mid, sg_out))
    loads = [pltpu.make_async_copy(src, dst, sem.at[0, i]) for i, (src, dst) in enumerate(into)]
    stores = [pltpu.make_async_copy(src, dst, sem.at[1, i]) for i, (src, dst) in enumerate(out)]
    for load in loads:
        load.start()
    for load, store in zip(loads, stores):
        load.wait()
        store.start()
    for store in stores:
        store.wait()


def side_of(devices):
    R = 1
    while 2 * R * R < devices:
        R += 1
    return R


def on_device(prev_out, next_grad, expert_ids, affinity, w_gate_up, w_down):
    slices = lax.axis_size("expert")
    sections = lax.axis_size("section")
    R = side_of(slices)
    rows, D = prev_out.shape[1:]
    top = expert_ids.shape[2]
    units = w_down.shape[2]
    H = D // 2
    block = 2 * rows
    split = slices // max(top, slices // 8)
    half = R // 2
    per = max(1, R // 4)
    groups = R // per
    vmem = pl.BlockSpec(memory_space=pltpu.VMEM)
    hbm = pl.BlockSpec(memory_space=pltpu.HBM)
    dma = pltpu.SemaphoreType.DMA
    flops = 2 * slices * rows * D * units * 6
    dx, gd, sg = pl.pallas_call(
        functools.partial(kernel, R, sections, split),
        out_shape=(
            jax.ShapeDtypeStruct((rows, D), BF16),
            jax.ShapeDtypeStruct((units, D), BF16),
            jax.ShapeDtypeStruct((rows, top), F32),
        ),
        in_specs=[hbm] * 6,
        out_specs=(vmem, vmem, vmem),
        scratch_shapes=[
            pltpu.VMEM((rows, D), BF16),
            pltpu.VMEM((rows, D), BF16),
            pltpu.VMEM((rows, top), jnp.int32),
            pltpu.VMEM((rows, top), F32),
            pltpu.VMEM((2, R, R, block, D + LANES), BF16),
            pltpu.VMEM((2, H, 2 * units), BF16),
            pltpu.VMEM((units, D), BF16),
            pltpu.VMEM((2, block, H), BF16),
            pltpu.VMEM((2, block, H), BF16),
            pltpu.VMEM((rows, LANES), F32),
            pltpu.VMEM((rows, LANES), F32),
            pltpu.VMEM((R, R, block, 2 * units), F32),
            pltpu.VMEM((R, R, block, units), F32),
            pltpu.VMEM((R, R, block, LANES), BF16),
            pltpu.VMEM((R, R, block, 2 * units), BF16),
            pltpu.VMEM((R, R, block, units), BF16),
            pltpu.VMEM((R, R, block, LANES), BF16),
            pltpu.VMEM((2, groups, per, block, H), F32),
            pltpu.VMEM((R, R, block, H), BF16),
            pltpu.VMEM((R, R, block, H), BF16),
            pltpu.VMEM((2, half + 1, groups, per, block, H + LANES), BF16),
            pltpu.VMEM((2, half + 1, groups, per, block, H + LANES), BF16),
            pltpu.VMEM((R, block, H + LANES), BF16),
            pltpu.VMEM((R, block, H + LANES), BF16),
            pltpu.VMEM((rows, H + LANES), F32),
            pltpu.VMEM((rows, H + LANES), F32),
            dma((6,)),
            dma((2,)),
            dma((2,)),
            dma((2,)),
            dma((2, half + 1)),
            dma((2, half + 1)),
            dma((2, half + 1)),
            dma((2, half + 1, R)),
            dma((R,)),
            dma((R,)),
            dma((R,)),
            dma((R,)),
            dma((2, half + 1)),
            dma((2, half + 1, groups)),
            dma((R,)),
            dma((R,)),
            dma((2,)),
        ],
        compiler_params=pltpu.CompilerParams(
            collective_id=0, has_side_effects=True, vmem_limit_bytes=VMEM_BYTES
        ),
        cost_estimate=pl.CostEstimate(flops=flops, bytes_accessed=4 * D * units * 2, transcendentals=0),
    )(
        prev_out[0],
        next_grad[0],
        expert_ids[0],
        affinity[0],
        w_gate_up[0, 0].reshape(2, H, 2 * units),
        w_down[0, 0],
    )
    dx, gd, sg = pl.pallas_call(
        finish,
        out_shape=(
            jax.ShapeDtypeStruct((rows, D), BF16),
            jax.ShapeDtypeStruct((units, D), BF16),
            jax.ShapeDtypeStruct((rows, top), F32),
        ),
        in_specs=[hbm] * 3,
        out_specs=(hbm,) * 3,
        scratch_shapes=[pltpu.VMEM((rows, D), BF16), pltpu.VMEM((units, D), BF16), pltpu.VMEM((rows, top), F32), dma((2, 3))],
        compiler_params=pltpu.CompilerParams(vmem_limit_bytes=VMEM_BYTES),
        cost_estimate=pl.CostEstimate(flops=0, bytes_accessed=4 * D * (units + rows), transcendentals=0),
    )(dx, gd, sg)
    return dx[None], gd[None, None], sg[None]


def solution(mesh):
    in_specs = (
        P("section", "expert", None),
        P("section", "expert", None),
        P("section", "expert", None),
        P("section", "expert", None),
        P("section", "expert", None, None),
        P("section", "expert", None, None),
    )
    out_specs = (
        P("section", "expert", None),
        P("section", "expert", None, None),
        P("section", "expert", None),
    )
    return jax.shard_map(
        on_device, mesh=mesh, in_specs=in_specs, out_specs=out_specs, check_vma=False
    )
```
